32 devices in a mesh: group: 2 (over x), rows: 16 (over z, y, core).
Axes of the slice: x: 2, y: 2, z: 4, core: 2. Of those that a mesh axis runs over, the one named last changes fastest.
Arguments:
- spectra: float32 [4, 1024, 6144], P('group', 'rows'), parts along dimension 0, may hold values from -6 to 6
- plane: float32 [1024, 6144], P('rows'), may hold values from -6 to 6
- interval_edges: int32 [12, 2], replicated, may hold values from 0 to 128
- tile_shifts: int32 [4, 12, 2], P('group'), parts along dimension 0, may hold values from -8 to 8, as said below
Outputs:
- correlation: float32 [4, 1024, 6144], P('group', 'rows'), parts along dimension 0
- aligned_spectra: float32 [4, 1024, 6144], P('group', 'rows'), parts along dimension 0
The draws below stay inside these ranges and needn't reach their ends.
There are 2 independent parts, one for each index of `group`. The reference program is written for one: setup_inputs(seed, part) draws one part's arguments, and reference() takes and returns one part's arrays. A program takes and returns all parts, laid end to end along the dimension named above; an argument that names none is the same for every part. Nothing has to cross between parts.
Inputs may be any that keep to these rules, and one draw needn't show every extreme that they name: `tile_shifts`: both shifts lie in -8 to 8; the 1024 shift equals 8 for some tile and -8 for another in every draw.
All inputs are finite; a program needn't handle non-finite values.
Results may differ from the reference program's by a relative error of at most 0.000098.
Values sent between devices are 32-bit elements; how exact they have to be, the bound alone decides.
A program may use at most 128 MiB of HBM per device.

```python
import jax
import jax.numpy as jnp
from jax import lax

F1 = 1024
F2 = 6144
TF2 = 512
MAXS = 8
SPEC = 2
T2 = 12


def draw_tile_shifts(key, part):
    first_key, second_key, third_key = jax.random.split(key, 3)
    total = SPEC * T2
    values = jax.random.randint(first_key, (total * 2,), -MAXS, MAXS + 1)
    first_slot = jax.random.randint(second_key, (), 0, total)
    spacing = jax.random.randint(third_key, (), 1, total)
    second_slot = (first_slot + spacing) % total
    values = values.at[2 * first_slot].set(MAXS)
    values = values.at[2 * second_slot].set(-MAXS)
    return values.reshape(SPEC, T2, 2).astype(jnp.int32)


def touch_ends(drawn, stream_key, smallest, high):
    longest = drawn.shape.index(max(drawn.shape))
    spots = []
    for shift in (0, 1):
        where = [jax.random.randint(jax.random.fold_in(stream_key, axis), (), 0, length) for axis, length in enumerate(drawn.shape)]
        where[longest] = (where[longest] + shift) % drawn.shape[longest]
        spots.append(tuple(where))
    return drawn.at[spots[0]].set(smallest).at[spots[1]].set(high)


def level_of(stream_key, extent, cuts, smallest, top_value):
    gain, own = 1.0, jax.random.fold_in(stream_key, 6)
    for position, parts in cuts:
        heights = jnp.exp(jax.random.uniform(jax.random.fold_in(own, position), (parts,), jnp.float32, smallest / len(cuts), top_value / len(cuts)))
        gain = gain * jnp.repeat(heights, extent[position] // parts).reshape([-1 if axis == position else 1 for axis in range(len(extent))])
    return gain


def bell_draw(rng, extent, width, limit, cuts=(), kind=jnp.bfloat16):
    drawn = jax.random.normal(rng, extent, jnp.float32) * width
    if len(cuts) > 0:
        drawn = level_of(rng, extent, cuts, -0.22, 0.18) * drawn
    return jnp.clip(drawn, min=-limit, max=limit).astype(kind)


def setup_inputs(seed: int = 0, part: int = 0) -> dict:
    seeds = jax.random.split(jax.random.key(seed), 5)
    own_keys = jax.random.split(jax.random.fold_in(seeds[4], part), 5)
    return {
        "spectra": bell_draw(own_keys[0], (SPEC, F1, F2), 1.0, 6.0, ((1, 16),), jnp.float32),
        "plane": bell_draw(seeds[1], (F1, F2), 1.0, 6.0, ((0, 16),), jnp.float32),
        "interval_edges": touch_ends(jax.random.randint(seeds[2], (T2, 2), 0, TF2 // 4 + 1), jax.random.fold_in(seeds[2], 1), 0, (TF2 // 4 + 1) - 1).astype(jnp.int32),
        "tile_shifts": draw_tile_shifts(jax.random.fold_in(jax.random.fold_in(seeds[4], part), 71), part),
    }


def interval_keep(interval_edges):
    column = jnp.arange(TF2, dtype=jnp.int32)[None, :]
    inside = (column >= interval_edges[:, 0:1]) & (column < TF2 - interval_edges[:, 1:2])
    return jnp.where(inside, 1.0, 0.0).astype(jnp.float32).reshape(F2)


def reference(spectra, plane, interval_edges, tile_shifts):
    keeper = interval_keep(interval_edges)
    plane_hat = jnp.fft.fft2(plane.reshape(F1, T2, TF2), axes=(0, 2))

    def correlate(single):
        single_hat = jnp.fft.fft2((single * keeper).reshape(F1, T2, TF2), axes=(0, 2))
        result = jnp.real(jnp.fft.ifft2(single_hat * jnp.conj(plane_hat), axes=(0, 2)))
        return (result * (float(F1 * TF2) ** -0.5)).reshape(F1, F2).astype(jnp.float32)

    correlation = lax.map(correlate, spectra)
    padded = jnp.pad(spectra, ((0, 0), (MAXS, MAXS), (MAXS, MAXS)))
    row_start = (MAXS - tile_shifts[:, :, 0]).astype(jnp.int32)
    col_start = (jnp.arange(T2, dtype=jnp.int32)[None, :] * TF2 + MAXS - tile_shifts[:, :, 1]).astype(jnp.int32)

    def cut_one(source, top_index, left_index):
        return lax.dynamic_slice(source, (top_index, left_index), (F1, TF2))

    def cut_spectrum(source, top_row, left_row):
        return jax.vmap(cut_one, in_axes=(None, 0, 0))(source, top_row, left_row)

    pieces = jax.vmap(cut_spectrum)(padded, row_start, col_start)
    aligned_spectra = jnp.transpose(pieces, (0, 2, 1, 3)).reshape(SPEC, F1, F2)
    return correlation, aligned_spectra
```

```python
import math

import jax
import jax.numpy as jnp
import numpy as np
from jax import lax
from jax.experimental import pallas as pl
from jax.experimental.pallas import tpu as pltpu
from jax.sharding import PartitionSpec as P

F1 = 1024
TF2 = 512
HALF = TF2 // 2
MAXS = 8
LANES = 128

exact = lax.Precision.HIGH
full = lax.Precision.HIGHEST


def trig(rows, columns, modulus):
    angle = np.outer(np.arange(rows), np.arange(columns)) % modulus * (2.0 * math.pi / modulus)
    return np.cos(angle), np.sin(angle)


def column_table():
    return np.stack(trig(F1, F1, F1))


def row_tables(span):
    groups = HALF // span
    cosine, sine = trig(TF2, HALF, TF2)
    alternate = np.where(np.arange(TF2) % 2 == 0, 1.0, -1.0)
    forward_imag = -sine
    forward_imag[:, 0] = alternate
    forward = np.stack([cosine, forward_imag], axis=1)
    forward = forward.reshape(TF2, 2, groups, span).transpose(0, 2, 1, 3)
    forward = forward.reshape(TF2, groups, 2 * span)
    weights = np.where(np.arange(HALF) == 0, 1.0, 2.0)[None, :]
    inverse_imag = -2.0 * sine
    inverse_imag[:, 0] = alternate
    inverse = np.stack([weights * cosine, inverse_imag], axis=1)
    inverse = inverse.reshape(TF2, 2, groups, span).transpose(2, 1, 3, 0)
    inverse = inverse.reshape(groups, 2 * span, TF2) * float(F1 * TF2) ** (-1.5)
    return forward, inverse


def align_kernel(shifts, body, above, below, out, padded):
    spectrum = pl.program_id(0)
    height, breadth = body.shape[1:]
    total = height + 2 * MAXS
    margin = jnp.zeros((total, LANES), jnp.float32)
    padded[:, :LANES] = margin
    padded[:, LANES + breadth :] = margin
    padded[:MAXS, LANES : LANES + breadth] = above[0]
    padded[MAXS : MAXS + height, LANES : LANES + breadth] = body[0]
    padded[MAXS + height :, LANES : LANES + breadth] = below[0]
    window = TF2 + 2 * LANES
    for tile in range(breadth // TF2):
        down = shifts[spectrum, tile, 0]
        right = shifts[spectrum, tile, 1]
        part = padded[:, tile * TF2 : tile * TF2 + window]
        part = pltpu.roll(part, lax.rem(right + window, window), 1)[:, LANES : LANES + TF2]
        part = pltpu.roll(part, lax.rem(down + total, total), 0)
        out[0, :, tile * TF2 : (tile + 1) * TF2] = part[MAXS : MAXS + height]


def aligned(spectra, tile_shifts):
    number, height, breadth = spectra.shape
    count = lax.axis_size("rows")
    head = spectra[:, :MAXS]
    tail = spectra[:, height - MAXS :]
    above = lax.ppermute(tail, "rows", [(i, i + 1) for i in range(count - 1)])
    below = lax.ppermute(head, "rows", [(i + 1, i) for i in range(count - 1)])
    whole = pl.BlockSpec((1, height, breadth), lambda s: (s, 0, 0))
    edge = pl.BlockSpec((1, MAXS, breadth), lambda s: (s, 0, 0))
    return pl.pallas_call(
        align_kernel,
        grid=(number,),
        out_shape=jax.ShapeDtypeStruct(spectra.shape, jnp.float32),
        in_specs=[pl.BlockSpec(memory_space=pltpu.SMEM), whole, edge, edge],
        out_specs=whole,
        scratch_shapes=[pltpu.VMEM((height + 2 * MAXS, breadth + 2 * LANES), jnp.float32)],
        compiler_params=pltpu.CompilerParams(vmem_limit_bytes=24 * 2**20),
        cost_estimate=pl.CostEstimate(
            flops=20 * spectra.size, bytes_accessed=8 * spectra.size, transcendentals=0
        ),
    )(tile_shifts, spectra, above, below)


def plain_products(plane_columns, received, packed):
    count, local, height, width = plane_columns.shape
    span = width // 2
    columns = column_table().astype(np.float32)

    def halves(block):
        pencil = block.transpose(0, 2, 1, 3).reshape(F1, local * width)
        both = jnp.einsum("pkn,nl->pkl", columns, pencil, precision=exact)
        return both.reshape(2, F1, local, 2, span)

    def spectrum_of(both):
        cosine, sine = both[0], both[1]
        return cosine[:, :, 0] + sine[:, :, 1], cosine[:, :, 1] - sine[:, :, 0]

    plane_halves = halves(plane_columns)
    plane_real, plane_imag = spectrum_of(plane_halves)

    def back(block):
        both = halves(block)
        real, imag = spectrum_of(both)
        out_real = real * plane_real + imag * plane_imag
        out_imag = imag * plane_real - real * plane_imag
        cosine, sine = both[0], both[1]
        pc, ps = plane_halves[0], plane_halves[1]
        mask = packed[None, :, None, :]
        first = jnp.stack([out_real, out_imag], axis=2)
        second = jnp.stack([-out_imag, out_real], axis=2)
        first = jnp.where(mask, cosine * pc + sine * ps, first)
        second = jnp.where(mask, sine * pc - cosine * ps, second)
        pair = jnp.stack([first, second]).reshape(2, F1, local * width)
        rows = jnp.einsum("pkn,pnl->kl", columns, pair, precision=exact)
        return rows.reshape(count, height, local, width).transpose(0, 2, 1, 3)

    return [back(block) for block in received]


def split(values):
    high = values.astype(jnp.bfloat16)
    return high, (values - high.astype(jnp.float32)).astype(jnp.bfloat16)


def product_3(table_high, table_low, rows, high, low):
    def dot(a, b):
        return jnp.dot(a, b, preferred_element_type=jnp.float32)

    top = table_high[rows, :]
    return dot(top, high) + (dot(top, low) + dot(table_low[rows, :], high))


CHUNK = 256


def forward_halves(table_high, table_low, block, both, high, low):
    count, local, height, width = block.shape
    for source in range(count):
        for part in range(local):
            rows = slice(source * height, (source + 1) * height)
            lanes = slice(part * width, (part + 1) * width)
            high[rows, lanes], low[rows, lanes] = split(block[source, part])

    @pl.loop(0, 2 * F1 // CHUNK)
    def _(step):
        rows = pl.ds(pl.multiple_of(step * CHUNK, CHUNK), CHUNK)
        both[rows, :] = product_3(table_high, table_low, rows, high[...], low[...])


def product_kernel(
    table_high, table_low, block, plane_both, packed, out, both, high, low, pair_high, pair_low
):
    count, local, height, width = block.shape
    forward_halves(table_high, table_low, block, both, high, low)
    rows_per = 64
    lane = lax.broadcasted_iota(jnp.int32, (rows_per, width), 1)
    is_real = lane < width // 2
    sign = jnp.where(is_real, 1.0, -1.0).astype(jnp.float32)

    def swap(values):
        return pltpu.roll(values, width // 2, 1)

    @pl.loop(0, F1 // rows_per)
    def _(step):
        top = pl.ds(pl.multiple_of(step * rows_per, rows_per), rows_per)
        bottom = pl.ds(pl.multiple_of(F1 + step * rows_per, rows_per), rows_per)
        for part in range(local):
            lanes = slice(part * width, (part + 1) * width)
            c, s = both[top, lanes], both[bottom, lanes]
            pc, ps = plane_both[top, lanes], plane_both[bottom, lanes]
            value = c + sign * swap(s)
            plane_value = pc + sign * swap(ps)
            same = value * plane_value
            cross = swap(value) * plane_value
            product = jnp.where(is_real, same + swap(same), swap(cross) - cross)
            alone = packed[0:1, lanes] > 0.5
            first = jnp.where(alone, c * pc + s * ps, product)
            second = jnp.where(alone, s * pc - c * ps, -sign * swap(product))
            pair_high[top, lanes], pair_low[top, lanes] = split(first)
            pair_high[bottom, lanes], pair_low[bottom, lanes] = split(second)

    per_step = CHUNK // height

    @pl.loop(0, F1 // CHUNK)
    def _(step):
        total = jnp.zeros((CHUNK, local * width), jnp.float32)
        for side in range(2):
            rows = pl.ds(pl.multiple_of(side * F1 + step * CHUNK, CHUNK), CHUNK)
            own = slice(side * F1, (side + 1) * F1)
            total += product_3(table_high, table_low, rows, pair_high[own], pair_low[own])
        for place in range(per_step):
            for part in range(local):
                out[step * per_step + place, part] = total[
                    place * height : (place + 1) * height, part * width : (part + 1) * width
                ]


def column_parts():
    return split_table(column_table().reshape(2 * F1, F1))


def kernel_plane(plane_columns):
    breadth = plane_columns.shape[1] * plane_columns.shape[3]
    space = pl.BlockSpec(memory_space=pltpu.VMEM)
    return pl.pallas_call(
        forward_halves,
        out_shape=jax.ShapeDtypeStruct((2 * F1, breadth), jnp.float32),
        in_specs=[space] * 3,
        out_specs=space,
        scratch_shapes=[pltpu.VMEM((F1, breadth), jnp.bfloat16)] * 2,
        compiler_params=pltpu.CompilerParams(vmem_limit_bytes=44 * 2**20),
        cost_estimate=pl.CostEstimate(
            flops=12 * F1 * F1 * breadth, bytes_accessed=8 * F1 * F1, transcendentals=0
        ),
    )(*column_parts(), plane_columns)


def kernel_products(plane_both, received, packed):
    breadth = plane_both.shape[1]
    lanes = jnp.stack([packed, packed], axis=1).reshape(1, breadth).astype(jnp.float32)
    space = pl.BlockSpec(memory_space=pltpu.VMEM)
    halves_shape = (2 * F1, breadth)
    call = pl.pallas_call(
        product_kernel,
        out_shape=jax.ShapeDtypeStruct(received[0].shape, jnp.float32),
        in_specs=[space] * 5,
        out_specs=space,
        scratch_shapes=[pltpu.VMEM(halves_shape, jnp.float32)]
        + [pltpu.VMEM((F1, breadth), jnp.bfloat16)] * 2
        + [pltpu.VMEM(halves_shape, jnp.bfloat16)] * 2,
        compiler_params=pltpu.CompilerParams(vmem_limit_bytes=44 * 2**20),
        cost_estimate=pl.CostEstimate(
            flops=24 * F1 * F1 * breadth, bytes_accessed=8 * F1 * F1, transcendentals=0
        ),
    )
    return [call(*column_parts(), block, plane_both, lanes) for block in received]


def product_of(values, table_high, table_low):
    high, low = split(values)

    def dot(a, b):
        return jnp.dot(a, b, preferred_element_type=jnp.float32)

    count = values.shape[0]
    both = dot(jnp.concatenate([high, low], axis=0), table_high)
    return both[:count] + (both[count:] + dot(high, table_low))


def bins_kernel(keeper, rows, table_high, table_low, out):
    height, breadth = rows.shape
    groups = TF2 // LANES
    values = rows[...] * keeper[...]
    tiles = [values[:, start : start + TF2] for start in range(0, breadth, TF2)]
    bins = product_of(jnp.concatenate(tiles, axis=0), table_high[...], table_low[...])
    for tile in range(len(tiles)):
        for group in range(groups):
            out[tile * groups + group] = bins[
                tile * height : (tile + 1) * height, group * LANES : (group + 1) * LANES
            ]


def rows_kernel(*refs):
    blocks, (table_high, table_low, out) = refs[:-3], refs[-3:]
    granules, height = blocks[0].shape[:2]
    groups = TF2 // LANES
    places = [(s, t) for s in range(len(blocks)) for t in range(granules // groups)]
    parts = [
        jnp.concatenate([blocks[s][t * groups + group] for group in range(groups)], axis=1)
        for s, t in places
    ]
    rows = product_of(jnp.concatenate(parts, axis=0), table_high[...], table_low[...])
    for place, (s, t) in enumerate(places):
        out[s, :, t * TF2 : (t + 1) * TF2] = rows[place * height : (place + 1) * height]


def tiles_at_once(tiles):
    return 3 if tiles % 3 == 0 else 2 if tiles % 2 == 0 else 1


def split_table(table):
    high = table.astype(jnp.bfloat16)
    return high, (table - high.astype(np.float64)).astype(jnp.bfloat16)


def kernel_bins(spectra, index, keeper, table):
    height, breadth = spectra.shape[1:]
    tiles, groups = breadth // TF2, TF2 // LANES
    step = tiles_at_once(tiles)
    fixed = pl.BlockSpec((TF2, TF2), lambda b: (0, 0))
    return pl.pallas_call(
        bins_kernel,
        grid=(tiles // step,),
        out_shape=jax.ShapeDtypeStruct((tiles * groups, height, LANES), jnp.float32),
        in_specs=[
            pl.BlockSpec((1, step * TF2), lambda b: (0, b)),
            pl.BlockSpec((None, height, step * TF2), lambda b: (index, 0, b)),
            fixed,
            fixed,
        ],
        out_specs=pl.BlockSpec((step * groups, height, LANES), lambda b: (b, 0, 0)),
        compiler_params=pltpu.CompilerParams(vmem_limit_bytes=24 * 2**20),
        cost_estimate=pl.CostEstimate(
            flops=6 * height * breadth * TF2, bytes_accessed=8 * height * breadth, transcendentals=0
        ),
    )(keeper, spectra, *split_table(table))


def kernel_rows(blocks, table):
    granules, height = blocks[0].shape[:2]
    groups = TF2 // LANES
    tiles = granules // groups
    number = len(blocks)
    step = tiles_at_once(tiles)
    fixed = pl.BlockSpec((TF2, TF2), lambda b: (0, 0))
    return pl.pallas_call(
        rows_kernel,
        grid=(tiles // step,),
        out_shape=jax.ShapeDtypeStruct((number, height, tiles * TF2), jnp.float32),
        in_specs=[pl.BlockSpec((step * groups, height, LANES), lambda b: (b, 0, 0))] * number
        + [fixed, fixed],
        out_specs=pl.BlockSpec((number, height, step * TF2), lambda b: (0, 0, b)),
        compiler_params=pltpu.CompilerParams(vmem_limit_bytes=24 * 2**20),
    )(*blocks, *split_table(table))


FOLD = F1 // 2
TILE_GROUPS = TF2 // LANES
BLOCK = 256
STRIP = 64
MESH_ID = pl.DeviceIdType.MESH


def folded_table():
    cosine, sine = trig(FOLD, F1, F1)
    sine[0] = np.where(np.arange(F1) % 2 == 0, 1.0, -1.0)
    return np.concatenate([cosine, sine])


def swapped(values):
    return pltpu.roll(values, LANES // 2, 1)


def whole_kernel(
    edges,
    shifts,
    spectra,
    plane,
    row_high_in,
    row_low_in,
    col_high_in,
    col_low_in,
    back_high_in,
    back_low_in,
    last_high_in,
    last_low_in,
    correlation,
    aligned_out,
    row_high,
    row_low,
    col_high,
    col_low,
    back_high,
    back_low,
    last_high,
    last_low,
    padded,
    plane_rows,
    plane_sent,
    plane_got,
    sent,
    got,
    returned,
    bins,
    coefs,
    both,
    high,
    low,
    pair_high,
    pair_low,
    load_sem,
    halo_send,
    halo_got,
    plane_send_sem,
    plane_got_sem,
    swap_send_sem,
    swap_got_sem,
    spec_send_sem,
    spec_got_sem,
    back_send_sem,
    back_got_sem,
):
    number, height, breadth = spectra.shape
    count = lax.axis_size("rows")
    chunks = breadth // LANES // count
    per_chunk = count // TILE_GROUPS
    share = plane_rows.shape[0]
    me = lax.axis_index("rows")
    side = lax.axis_index("group")
    other = 1 - side
    middle = slice(LANES, LANES + breadth)

    def load(source, target, sem):
        copy = pltpu.make_async_copy(source, target, load_sem.at[sem])
        copy.start()
        return copy

    own = pl.ds(pl.multiple_of(side * share, share), share)
    loads = [
        load(plane.at[own], plane_rows, 0),
        load(row_high_in, row_high, 1),
        load(row_low_in, row_low, 2),
        load(spectra, padded.at[:, pl.ds(MAXS, height), pl.ds(LANES, breadth)], 3),
        load(col_high_in, col_high, 4),
        load(col_low_in, col_low, 5),
        load(back_high_in, back_high, 6),
        load(back_low_in, back_low, 7),
        load(last_high_in, last_high, 8),
        load(last_low_in, last_low, 9),
    ]

    barrier = pltpu.get_barrier_semaphore()

    def greet(step, carry):
        peer = lax.rem(me + step, count)
        pl.semaphore_signal(barrier, 1, device_id=(side, peer), device_id_type=MESH_ID)
        return carry

    lax.fori_loop(1, count, greet, 0)
    pl.semaphore_signal(barrier, 1, device_id=(other, me), device_id_type=MESH_ID)
    pl.semaphore_wait(barrier, count)

    def remote(source, target, send, got_sem, where):
        return pltpu.make_async_remote_copy(
            src_ref=source,
            dst_ref=target,
            send_sem=send,
            recv_sem=got_sem,
            device_id=where,
            device_id_type=MESH_ID,
        )

    def halo_down():
        return remote(
            spectra.at[:, pl.ds(height - MAXS, MAXS)],
            padded.at[:, pl.ds(0, MAXS), pl.ds(LANES, breadth)],
            halo_send.at[0],
            halo_got.at[0],
            (side, lax.rem(me + 1, count)),
        )

    def halo_up():
        return remote(
            spectra.at[:, pl.ds(0, MAXS)],
            padded.at[:, pl.ds(MAXS + height, MAXS), pl.ds(LANES, breadth)],
            halo_send.at[1],
            halo_got.at[1],
            (side, lax.rem(me + count - 1, count)),
        )

    @pl.when(me < count - 1)
    def _():
        halo_down().start()

    @pl.when(me > 0)
    def _():
        halo_up().start()

    def far_first(step, carry, start):
        half = lax.div(step + 1, 2)
        offset = count // 2 + half * (1 - 2 * lax.rem(step, 2))
        start(lax.rem(me + offset, count))
        return carry

    def to_all(start):
        lax.fori_loop(0, count - 1, lambda step, carry: far_first(step, carry, start), 0)

    loads[0].wait()
    loads[1].wait()
    loads[2].wait()
    for chunk in range(chunks):

        def bins_of(rows, table_high, table_low):
            return product_of(rows, table_high[...], table_low[...])

        tiles = [
            plane_rows[:, start : start + TF2]
            for start in range(chunk * per_chunk * TF2, (chunk + 1) * per_chunk * TF2, TF2)
        ]
        found = bins_of(jnp.concatenate(tiles, axis=0), row_high, row_low)
        for tile in range(per_chunk):
            for group in range(TILE_GROUPS):
                plane_sent[chunk, tile * TILE_GROUPS + group] = found[
                    tile * share : (tile + 1) * share, group * LANES : (group + 1) * LANES
                ]
        plane_got[chunk, me, own] = plane_sent[chunk, me]

        def send_plane(peer):
            remote(
                plane_sent.at[chunk, peer],
                plane_got.at[chunk, me, own],
                plane_send_sem.at[chunk],
                plane_got_sem.at[chunk],
                (side, peer),
            ).start()

        to_all(send_plane)

    loads[3].wait()
    column = lax.broadcasted_iota(jnp.int32, (1, TF2), 1)
    for chunk in range(chunks):

        def spectrum_bins(spectrum, carry):
            parts = []
            for tile in range(chunk * per_chunk, (chunk + 1) * per_chunk):
                inside = (column >= edges[tile, 0]) & (column < TF2 - edges[tile, 1])
                keeper = jnp.where(inside, 1.0, 0.0).astype(jnp.float32)
                lanes = slice(LANES + tile * TF2, LANES + (tile + 1) * TF2)
                parts.append(padded[spectrum, MAXS : MAXS + height, lanes] * keeper)
            found = product_of(jnp.concatenate(parts, axis=0), row_high[...], row_low[...])
            for tile in range(per_chunk):
                for group in range(TILE_GROUPS):
                    sent[chunk, spectrum, tile * TILE_GROUPS + group] = found[
                        tile * height : (tile + 1) * height, group * LANES : (group + 1) * LANES
                    ]
            got[chunk, spectrum, me] = sent[chunk, spectrum, me]

            def send_spectrum(peer):
                remote(
                    sent.at[chunk, spectrum, peer],
                    got.at[chunk, spectrum, me],
                    spec_send_sem.at[chunk, spectrum],
                    spec_got_sem.at[chunk, spectrum],
                    (side, peer),
                ).start()

            to_all(send_spectrum)
            return carry

        lax.fori_loop(0, number, spectrum_bins, 0)

    total = height + 2 * MAXS
    margin = jnp.zeros((number, total, LANES), jnp.float32)
    padded[:, :, :LANES] = margin
    padded[:, :, LANES + breadth :] = margin
    blank = jnp.zeros((number, MAXS, breadth), jnp.float32)

    @pl.when(me == 0)
    def _():
        padded[:, :MAXS, middle] = blank

    @pl.when(me == count - 1)
    def _():
        padded[:, MAXS + height :, middle] = blank

    @pl.when(me > 0)
    def _():
        halo_down().wait_recv()

    @pl.when(me < count - 1)
    def _():
        halo_up().wait_recv()

    window = TF2 + 2 * LANES
    for spectrum in range(number):

        @pl.loop(0, breadth // TF2)
        def _(tile):
            down = shifts[spectrum, tile, 0]
            right = shifts[spectrum, tile, 1]
            start = pl.multiple_of(tile * TF2, TF2)
            part = padded[spectrum, :, pl.ds(start, window)]
            part = pltpu.roll(part, lax.rem(right + window, window), 1)[:, LANES : LANES + TF2]
            part = pltpu.roll(part, lax.rem(down + total, total), 0)
            aligned_out[spectrum, :, pl.ds(start, TF2)] = part[MAXS : MAXS + height]

    def landed(buffer, sem):
        fifteen = buffer.at[pl.ds(0, count - 1)]
        pltpu.make_async_copy(fifteen, fifteen, sem).wait()

    def swap_plane(chunk):
        half = plane_got.at[chunk, :, own]
        return remote(
            half, half, swap_send_sem.at[chunk], swap_got_sem.at[chunk], (other, me)
        )

    for chunk in range(chunks):
        landed(plane_sent.at[chunk], plane_got_sem.at[chunk])
        swap_plane(chunk).start()

    def transform(width):
        @pl.loop(0, F1 // BLOCK)
        def _(step):
            rows = pl.ds(pl.multiple_of(step * BLOCK, BLOCK), BLOCK)
            both[rows, :width] = product_3(
                col_high, col_low, rows, high[:, :width], low[:, :width]
            )

    for load_index in range(4, 10):
        loads[load_index].wait()

    lane = lax.broadcasted_iota(jnp.int32, (STRIP, LANES), 1)
    is_real = lane < LANES // 2
    first_row = lax.broadcasted_iota(jnp.int32, (STRIP, LANES), 0) == 0
    alone = (lax.rem(lane, LANES // 2) == 0) & (lax.rem(me, TILE_GROUPS) == 0)

    def strips(body):
        @pl.loop(0, FOLD // STRIP)
        def _(step):
            start = pl.multiple_of(step * STRIP, STRIP)
            body(pl.ds(start, STRIP), pl.ds(FOLD + start, STRIP))

    zero = jnp.zeros((STRIP, LANES), jnp.float32)

    def plane_coefs(chunk):
        def body(top, bottom):
            c, s = both[top, :LANES], both[bottom, :LANES]
            sc, ss = swapped(c), swapped(s)
            c2, s2 = c + c, s + s
            coefs[chunk, 0, top, :] = jnp.where(alone | is_real, c2, sc + sc)
            coefs[chunk, 1, top, :] = jnp.where(alone, zero, jnp.where(is_real, sc + sc, -c2))
            coefs[chunk, 2, top, :] = jnp.where(alone | is_real, s2, ss + ss)
            coefs[chunk, 3, top, :] = jnp.where(alone, zero, jnp.where(is_real, ss + ss, -s2))

        strips(body)

    def store_pair(rows, lanes, values, high_ref, low_ref):
        high_ref[rows, lanes], low_ref[rows, lanes] = split(values)

    def pairs(chunk):
        for spectrum in range(number):
            lanes = slice(spectrum * LANES, (spectrum + 1) * LANES)

            def take(top, bottom):
                c, s = both[top, lanes], both[bottom, lanes]
                sc, ss = swapped(c), swapped(s)
                a, d = coefs[chunk, 0, top, :], coefs[chunk, 1, top, :]
                f, b = coefs[chunk, 2, top, :], coefs[chunk, 3, top, :]
                return c, s, sc, ss, a, d, f, b

            def body(top, bottom):
                c, s, sc, ss, a, d, f, b = take(top, bottom)
                store_pair(top, lanes, (c * a + sc * d) + (s * f + ss * b), pair_high, pair_low)
                store_pair(bottom, lanes, (s * a + ss * d) - (c * f + sc * b), pair_high, pair_low)

            strips(body)
            top, bottom = pl.ds(0, STRIP), pl.ds(FOLD, STRIP)
            c, s, sc, ss, a, d, f, b = take(top, bottom)
            zeroth = 0.5 * (c * a + sc * d)
            nyquist = 0.5 * (s * f + ss * b)
            first = (c * a + sc * d) + (s * f + ss * b)
            second = (s * a + ss * d) - (c * f + sc * b)
            store_pair(top, lanes, jnp.where(first_row, zeroth, first), pair_high, pair_low)
            store_pair(bottom, lanes, jnp.where(first_row, nyquist, second), pair_high, pair_low)

    def gather(block, lanes):
        @pl.loop(0, count)
        def _(source):
            rows = pl.ds(pl.multiple_of(source * height, height), height)
            high[rows, lanes], low[rows, lanes] = split(block[source])

    for chunk in range(chunks):
        swapped_half = plane_got.at[chunk, :, pl.ds(pl.multiple_of(other * share, share), share)]
        pltpu.make_async_copy(swapped_half, swapped_half, swap_got_sem.at[chunk]).wait()
        gather(plane_got.at[chunk], slice(0, LANES))
        transform(LANES)
        plane_coefs(chunk)

    for chunk in range(chunks):
        for spectrum in range(number):
            landed(got.at[chunk, spectrum], spec_got_sem.at[chunk, spectrum])
            gather(got.at[chunk, spectrum], slice(spectrum * LANES, (spectrum + 1) * LANES))
        transform(number * LANES)
        pairs(chunk)
        held = BLOCK // height

        def back(step, carry):
            place = lax.rem(lax.div(me, held) + count // held // 2 + step, count // held)
            rows = pl.ds(pl.multiple_of(place * BLOCK, BLOCK), BLOCK)
            values = product_3(back_high, back_low, rows, pair_high[...], pair_low[...])
            for spectrum in range(number):
                for part in range(held):
                    returned[chunk, spectrum, place * held + part] = values[
                        part * height : (part + 1) * height,
                        spectrum * LANES : (spectrum + 1) * LANES,
                    ]

            def send_back(index, inner):
                spectrum = lax.div(index, held)
                peer = place * held + lax.rem(index, held)

                @pl.when(peer != me)
                def _():
                    remote(
                        returned.at[chunk, spectrum, peer],
                        bins.at[chunk, spectrum, me],
                        back_send_sem.at[chunk, spectrum],
                        back_got_sem.at[chunk, spectrum],
                        (side, peer),
                    ).start()

                return inner

            lax.fori_loop(0, number * held, send_back, 0)
            return carry

        lax.fori_loop(0, count // held, back, 0)
        for spectrum in range(number):
            bins[chunk, spectrum, me] = returned[chunk, spectrum, me]

    for chunk in range(chunks):
        for spectrum in range(number):
            landed(bins.at[chunk, spectrum], back_got_sem.at[chunk, spectrum])
            parts = [
                jnp.concatenate(
                    [
                        bins[chunk, spectrum, tile * TILE_GROUPS + group]
                        for group in range(TILE_GROUPS)
                    ],
                    axis=1,
                )
                for tile in range(per_chunk)
            ]
            values = product_of(jnp.concatenate(parts, axis=0), last_high[...], last_low[...])
            for tile in range(per_chunk):
                start = (chunk * per_chunk + tile) * TF2
                correlation[spectrum, :, start : start + TF2] = values[
                    tile * height : (tile + 1) * height
                ]

    for chunk in range(chunks):
        landed(plane_sent.at[chunk], plane_send_sem.at[chunk])
        swap_plane(chunk).wait_send()
        for spectrum in range(number):
            landed(sent.at[chunk, spectrum], spec_send_sem.at[chunk, spectrum])
            landed(returned.at[chunk, spectrum], back_send_sem.at[chunk, spectrum])

    @pl.when(me < count - 1)
    def _():
        halo_down().wait_send()

    @pl.when(me > 0)
    def _():
        halo_up().wait_send()


def kernel_whole(spectra, plane, interval_edges, tile_shifts, forward, inverse):
    number, height, breadth = spectra.shape
    count = lax.axis_size("rows")
    share = height // lax.axis_size("group")
    chunks = breadth // LANES // count
    columns = folded_table()
    tables = (
        *split_table(forward),
        *split_table(columns),
        *split_table(np.ascontiguousarray(columns.T)),
        *split_table(inverse),
    )
    small = pl.BlockSpec(memory_space=pltpu.SMEM)
    far = pl.BlockSpec(memory_space=pl.ANY)
    near = pl.BlockSpec(memory_space=pltpu.VMEM)
    whole = jax.ShapeDtypeStruct(spectra.shape, jnp.float32)
    breadths = (F1, number * LANES)
    blocks = (chunks, number, count, height, LANES)
    return pl.pallas_call(
        whole_kernel,
        out_shape=(whole, whole),
        in_specs=[small, small] + [far] * (2 + len(tables)),
        out_specs=(near, near),
        scratch_shapes=[pltpu.VMEM(table.shape, jnp.bfloat16) for table in tables]
        + [
            pltpu.VMEM((number, height + 2 * MAXS, breadth + 2 * LANES), jnp.float32),
            pltpu.VMEM((share, breadth), jnp.float32),
            pltpu.VMEM((chunks, count, share, LANES), jnp.float32),
            pltpu.VMEM((chunks, count, height, LANES), jnp.float32),
            pltpu.VMEM(blocks, jnp.float32),
            pltpu.VMEM(blocks, jnp.float32),
            pltpu.VMEM(blocks, jnp.float32),
            pltpu.VMEM(blocks, jnp.float32),
            pltpu.VMEM((chunks, 4, FOLD, LANES), jnp.float32),
            pltpu.VMEM(breadths, jnp.float32),
            pltpu.VMEM(breadths, jnp.bfloat16),
            pltpu.VMEM(breadths, jnp.bfloat16),
            pltpu.VMEM(breadths, jnp.bfloat16),
            pltpu.VMEM(breadths, jnp.bfloat16),
            pltpu.SemaphoreType.DMA((10,)),
            pltpu.SemaphoreType.DMA((2,)),
            pltpu.SemaphoreType.DMA((2,)),
            pltpu.SemaphoreType.DMA((chunks,)),
            pltpu.SemaphoreType.DMA((chunks,)),
            pltpu.SemaphoreType.DMA((chunks,)),
            pltpu.SemaphoreType.DMA((chunks,)),
            pltpu.SemaphoreType.DMA((chunks, number)),
            pltpu.SemaphoreType.DMA((chunks, number)),
            pltpu.SemaphoreType.DMA((chunks, number)),
            pltpu.SemaphoreType.DMA((chunks, number)),
        ],
        compiler_params=pltpu.CompilerParams(
            collective_id=0, has_side_effects=True, vmem_limit_bytes=48 * 2**20
        ),
        cost_estimate=pl.CostEstimate(
            flops=2 * 3 * F1 * F1 * (2 * number + 2) * chunks * LANES,
            bytes_accessed=16 * spectra.size,
            transcendentals=0,
        ),
    )(interval_edges, tile_shifts, spectra, plane, *tables)


def per_device(spectra, plane, interval_edges, tile_shifts):
    number, height, breadth = spectra.shape
    count = lax.axis_size("rows")
    tiles = breadth // TF2
    span = math.gcd(breadth // 2 // count, HALF)
    groups = HALF // span
    width = 2 * span
    local = tiles * groups // count
    forward, inverse = row_tables(span)

    point = jnp.arange(TF2, dtype=jnp.int32)[None, :]
    inside = (point >= interval_edges[:, 0:1]) & (point < TF2 - interval_edges[:, 1:2])
    keeper = jnp.where(inside, 1.0, 0.0).astype(jnp.float32).reshape(1, breadth)

    cohorts = lax.axis_size("group")
    share = height // cohorts
    whole_tiles = width == LANES and share % 16 == 0
    if whole_tiles and cohorts == 2 and height * count == F1 and count % groups == 0:
        tables = (forward.reshape(TF2, TF2), inverse.reshape(TF2, TF2))
        return kernel_whole(spectra, plane, interval_edges, tile_shifts, *tables)

    def to_columns(rows, index, kept, after=None):
        held = rows.shape[1]
        if whole_tiles:
            bins = kernel_bins(rows, index, kept, forward.reshape(TF2, TF2))
        else:
            blocks = (rows[index] * kept).reshape(held, tiles, TF2)
            table = forward.astype(np.float32)
            bins = jnp.einsum("rbn,njl->bjrl", blocks, table, precision=full)
        sent = bins.reshape(count, local, held, width)
        if after is not None:
            sent, _ = lax.optimization_barrier((sent, after))
        return lax.all_to_all(sent, "rows", split_axis=0, concat_axis=0, tiled=True)

    granule = lax.axis_index("rows") * local + jnp.arange(local, dtype=jnp.int32)
    packed = (granule % groups == 0)[:, None] & (jnp.arange(span) == 0)[None, :]
    own = lax.axis_index("group")
    plane_rows = lax.dynamic_slice_in_dim(plane, own * share, share, axis=0)
    mine = to_columns(plane_rows[None], 0, jnp.ones_like(keeper))
    if cohorts == 2:
        other = lax.ppermute(mine, "group", [(0, 1), (1, 0)])
        ordered = [jnp.where(own == 0, mine, other), jnp.where(own == 0, other, mine)]
        plane_columns = jnp.concatenate(ordered, axis=2)
    else:
        plane_columns = lax.all_gather(mine, "group", axis=2, tiled=True)
    plane_both = kernel_plane(plane_columns) if whole_tiles else None
    received = [to_columns(spectra, s, keeper, plane_both if s else None) for s in range(number)]
    aligned_spectra = aligned(spectra, tile_shifts)
    if whole_tiles:
        products = kernel_products(plane_both, received, packed)
    else:
        products = plain_products(plane_columns, received, packed)
    returned = [
        lax.all_to_all(block, "rows", split_axis=0, concat_axis=0, tiled=True)
        for block in products
    ]

    if whole_tiles:
        blocks = [block.reshape(tiles * groups, height, width) for block in returned]
        return (kernel_rows(blocks, inverse.reshape(TF2, TF2)), aligned_spectra)

    def to_rows(block):
        bins = block.reshape(tiles, groups, height, width)
        table = inverse.astype(np.float32)
        return jnp.einsum("bjrl,jln->rbn", bins, table, precision=full).reshape(height, breadth)

    correlation = jnp.stack([to_rows(block) for block in returned])
    return (correlation, aligned_spectra)


def solution(mesh):
    placed = (P("group", "rows", None), P("rows", None), P(), P("group", None, None))
    return jax.shard_map(
        per_device,
        mesh=mesh,
        in_specs=placed,
        out_specs=(P("group", "rows", None), P("group", "rows", None)),
        check_vma=False,
    )
```

```python
import math

import jax
import jax.numpy as jnp
import numpy as np
from jax import lax
from jax.experimental import pallas as pl
from jax.experimental.pallas import tpu as pltpu
from jax.sharding import PartitionSpec as P

F1 = 1024
TF2 = 512
HALF = TF2 // 2
MAXS = 8
LANES = 128

exact = lax.Precision.HIGH
full = lax.Precision.HIGHEST


def trig(rows, columns, modulus):
    angle = np.outer(np.arange(rows), np.arange(columns)) % modulus * (2.0 * math.pi / modulus)
    return np.cos(angle), np.sin(angle)


def column_table():
    return np.stack(trig(F1, F1, F1))


def row_tables(span):
    groups = HALF // span
    cosine, sine = trig(TF2, HALF, TF2)
    alternate = np.where(np.arange(TF2) % 2 == 0, 1.0, -1.0)
    forward_imag = -sine
    forward_imag[:, 0] = alternate
    forward = np.stack([cosine, forward_imag], axis=1)
    forward = forward.reshape(TF2, 2, groups, span).transpose(0, 2, 1, 3)
    forward = forward.reshape(TF2, groups, 2 * span)
    weights = np.where(np.arange(HALF) == 0, 1.0, 2.0)[None, :]
    inverse_imag = -2.0 * sine
    inverse_imag[:, 0] = alternate
    inverse = np.stack([weights * cosine, inverse_imag], axis=1)
    inverse = inverse.reshape(TF2, 2, groups, span).transpose(2, 1, 3, 0)
    inverse = inverse.reshape(groups, 2 * span, TF2) * float(F1 * TF2) ** (-1.5)
    return forward, inverse


def align_kernel(shifts, body, above, below, out, padded):
    spectrum = pl.program_id(0)
    height, breadth = body.shape[1:]
    total = height + 2 * MAXS
    margin = jnp.zeros((total, LANES), jnp.float32)
    padded[:, :LANES] = margin
    padded[:, LANES + breadth :] = margin
    padded[:MAXS, LANES : LANES + breadth] = above[0]
    padded[MAXS : MAXS + height, LANES : LANES + breadth] = body[0]
    padded[MAXS + height :, LANES : LANES + breadth] = below[0]
    window = TF2 + 2 * LANES
    for tile in range(breadth // TF2):
        down = shifts[spectrum, tile, 0]
        right = shifts[spectrum, tile, 1]
        part = padded[:, tile * TF2 : tile * TF2 + window]
        part = pltpu.roll(part, lax.rem(right + window, window), 1)[:, LANES : LANES + TF2]
        part = pltpu.roll(part, lax.rem(down + total, total), 0)
        out[0, :, tile * TF2 : (tile + 1) * TF2] = part[MAXS : MAXS + height]


def aligned(spectra, tile_shifts):
    number, height, breadth = spectra.shape
    count = lax.axis_size("rows")
    head = spectra[:, :MAXS]
    tail = spectra[:, height - MAXS :]
    above = lax.ppermute(tail, "rows", [(i, i + 1) for i in range(count - 1)])
    below = lax.ppermute(head, "rows", [(i + 1, i) for i in range(count - 1)])
    whole = pl.BlockSpec((1, height, breadth), lambda s: (s, 0, 0))
    edge = pl.BlockSpec((1, MAXS, breadth), lambda s: (s, 0, 0))
    return pl.pallas_call(
        align_kernel,
        grid=(number,),
        out_shape=jax.ShapeDtypeStruct(spectra.shape, jnp.float32),
        in_specs=[pl.BlockSpec(memory_space=pltpu.SMEM), whole, edge, edge],
        out_specs=whole,
        scratch_shapes=[pltpu.VMEM((height + 2 * MAXS, breadth + 2 * LANES), jnp.float32)],
        compiler_params=pltpu.CompilerParams(vmem_limit_bytes=24 * 2**20),
        cost_estimate=pl.CostEstimate(
            flops=20 * spectra.size, bytes_accessed=8 * spectra.size, transcendentals=0
        ),
    )(tile_shifts, spectra, above, below)


def plain_products(plane_columns, received, packed):
    count, local, height, width = plane_columns.shape
    span = width // 2
    columns = column_table().astype(np.float32)

    def halves(block):
        pencil = block.transpose(0, 2, 1, 3).reshape(F1, local * width)
        both = jnp.einsum("pkn,nl->pkl", columns, pencil, precision=exact)
        return both.reshape(2, F1, local, 2, span)

    def spectrum_of(both):
        cosine, sine = both[0], both[1]
        return cosine[:, :, 0] + sine[:, :, 1], cosine[:, :, 1] - sine[:, :, 0]

    plane_halves = halves(plane_columns)
    plane_real, plane_imag = spectrum_of(plane_halves)

    def back(block):
        both = halves(block)
        real, imag = spectrum_of(both)
        out_real = real * plane_real + imag * plane_imag
        out_imag = imag * plane_real - real * plane_imag
        cosine, sine = both[0], both[1]
        pc, ps = plane_halves[0], plane_halves[1]
        mask = packed[None, :, None, :]
        first = jnp.stack([out_real, out_imag], axis=2)
        second = jnp.stack([-out_imag, out_real], axis=2)
        first = jnp.where(mask, cosine * pc + sine * ps, first)
        second = jnp.where(mask, sine * pc - cosine * ps, second)
        pair = jnp.stack([first, second]).reshape(2, F1, local * width)
        rows = jnp.einsum("pkn,pnl->kl", columns, pair, precision=exact)
        return rows.reshape(count, height, local, width).transpose(0, 2, 1, 3)

    return [back(block) for block in received]


def split(values):
    high = values.astype(jnp.bfloat16)
    return high, (values - high.astype(jnp.float32)).astype(jnp.bfloat16)


def product_3(table_high, table_low, rows, high, low):
    def dot(a, b):
        return jnp.dot(a, b, preferred_element_type=jnp.float32)

    top = table_high[rows, :]
    return dot(top, high) + (dot(top, low) + dot(table_low[rows, :], high))


CHUNK = 256


def forward_halves(table_high, table_low, block, both, high, low):
    count, local, height, width = block.shape
    for source in range(count):
        for part in range(local):
            rows = slice(source * height, (source + 1) * height)
            lanes = slice(part * width, (part + 1) * width)
            high[rows, lanes], low[rows, lanes] = split(block[source, part])

    @pl.loop(0, 2 * F1 // CHUNK)
    def _(step):
        rows = pl.ds(pl.multiple_of(step * CHUNK, CHUNK), CHUNK)
        both[rows, :] = product_3(table_high, table_low, rows, high[...], low[...])


def product_kernel(
    table_high, table_low, block, plane_both, packed, out, both, high, low, pair_high, pair_low
):
    count, local, height, width = block.shape
    forward_halves(table_high, table_low, block, both, high, low)
    rows_per = 64
    lane = lax.broadcasted_iota(jnp.int32, (rows_per, width), 1)
    is_real = lane < width // 2
    sign = jnp.where(is_real, 1.0, -1.0).astype(jnp.float32)

    def swap(values):
        return pltpu.roll(values, width // 2, 1)

    @pl.loop(0, F1 // rows_per)
    def _(step):
        top = pl.ds(pl.multiple_of(step * rows_per, rows_per), rows_per)
        bottom = pl.ds(pl.multiple_of(F1 + step * rows_per, rows_per), rows_per)
        for part in range(local):
            lanes = slice(part * width, (part + 1) * width)
            c, s = both[top, lanes], both[bottom, lanes]
            pc, ps = plane_both[top, lanes], plane_both[bottom, lanes]
            value = c + sign * swap(s)
            plane_value = pc + sign * swap(ps)
            same = value * plane_value
            cross = swap(value) * plane_value
            product = jnp.where(is_real, same + swap(same), swap(cross) - cross)
            alone = packed[0:1, lanes] > 0.5
            first = jnp.where(alone, c * pc + s * ps, product)
            second = jnp.where(alone, s * pc - c * ps, -sign * swap(product))
            pair_high[top, lanes], pair_low[top, lanes] = split(first)
            pair_high[bottom, lanes], pair_low[bottom, lanes] = split(second)

    per_step = CHUNK // height

    @pl.loop(0, F1 // CHUNK)
    def _(step):
        total = jnp.zeros((CHUNK, local * width), jnp.float32)
        for side in range(2):
            rows = pl.ds(pl.multiple_of(side * F1 + step * CHUNK, CHUNK), CHUNK)
            own = slice(side * F1, (side + 1) * F1)
            total += product_3(table_high, table_low, rows, pair_high[own], pair_low[own])
        for place in range(per_step):
            for part in range(local):
                out[step * per_step + place, part] = total[
                    place * height : (place + 1) * height, part * width : (part + 1) * width
                ]


def column_parts():
    return split_table(column_table().reshape(2 * F1, F1))


def kernel_plane(plane_columns):
    breadth = plane_columns.shape[1] * plane_columns.shape[3]
    space = pl.BlockSpec(memory_space=pltpu.VMEM)
    return pl.pallas_call(
        forward_halves,
        out_shape=jax.ShapeDtypeStruct((2 * F1, breadth), jnp.float32),
        in_specs=[space] * 3,
        out_specs=space,
        scratch_shapes=[pltpu.VMEM((F1, breadth), jnp.bfloat16)] * 2,
        compiler_params=pltpu.CompilerParams(vmem_limit_bytes=44 * 2**20),
        cost_estimate=pl.CostEstimate(
            flops=12 * F1 * F1 * breadth, bytes_accessed=8 * F1 * F1, transcendentals=0
        ),
    )(*column_parts(), plane_columns)


def kernel_products(plane_both, received, packed):
    breadth = plane_both.shape[1]
    lanes = jnp.stack([packed, packed], axis=1).reshape(1, breadth).astype(jnp.float32)
    space = pl.BlockSpec(memory_space=pltpu.VMEM)
    halves_shape = (2 * F1, breadth)
    call = pl.pallas_call(
        product_kernel,
        out_shape=jax.ShapeDtypeStruct(received[0].shape, jnp.float32),
        in_specs=[space] * 5,
        out_specs=space,
        scratch_shapes=[pltpu.VMEM(halves_shape, jnp.float32)]
        + [pltpu.VMEM((F1, breadth), jnp.bfloat16)] * 2
        + [pltpu.VMEM(halves_shape, jnp.bfloat16)] * 2,
        compiler_params=pltpu.CompilerParams(vmem_limit_bytes=44 * 2**20),
        cost_estimate=pl.CostEstimate(
            flops=24 * F1 * F1 * breadth, bytes_accessed=8 * F1 * F1, transcendentals=0
        ),
    )
    return [call(*column_parts(), block, plane_both, lanes) for block in received]


def product_of(values, table_high, table_low):
    high, low = split(values)

    def dot(a, b):
        return jnp.dot(a, b, preferred_element_type=jnp.float32)

    count = values.shape[0]
    both = dot(jnp.concatenate([high, low], axis=0), table_high)
    return both[:count] + (both[count:] + dot(high, table_low))


def bins_kernel(keeper, rows, table_high, table_low, out):
    height, breadth = rows.shape
    groups = TF2 // LANES
    values = rows[...] * keeper[...]
    tiles = [values[:, start : start + TF2] for start in range(0, breadth, TF2)]
    bins = product_of(jnp.concatenate(tiles, axis=0), table_high[...], table_low[...])
    for tile in range(len(tiles)):
        for group in range(groups):
            out[tile * groups + group] = bins[
                tile * height : (tile + 1) * height, group * LANES : (group + 1) * LANES
            ]


def rows_kernel(*refs):
    blocks, (table_high, table_low, out) = refs[:-3], refs[-3:]
    granules, height = blocks[0].shape[:2]
    groups = TF2 // LANES
    places = [(s, t) for s in range(len(blocks)) for t in range(granules // groups)]
    parts = [
        jnp.concatenate([blocks[s][t * groups + group] for group in range(groups)], axis=1)
        for s, t in places
    ]
    rows = product_of(jnp.concatenate(parts, axis=0), table_high[...], table_low[...])
    for place, (s, t) in enumerate(places):
        out[s, :, t * TF2 : (t + 1) * TF2] = rows[place * height : (place + 1) * height]


def tiles_at_once(tiles):
    return 3 if tiles % 3 == 0 else 2 if tiles % 2 == 0 else 1


def split_table(table):
    high = table.astype(jnp.bfloat16)
    return high, (table - high.astype(np.float64)).astype(jnp.bfloat16)


def kernel_bins(spectra, index, keeper, table):
    height, breadth = spectra.shape[1:]
    tiles, groups = breadth // TF2, TF2 // LANES
    step = tiles_at_once(tiles)
    fixed = pl.BlockSpec((TF2, TF2), lambda b: (0, 0))
    return pl.pallas_call(
        bins_kernel,
        grid=(tiles // step,),
        out_shape=jax.ShapeDtypeStruct((tiles * groups, height, LANES), jnp.float32),
        in_specs=[
            pl.BlockSpec((1, step * TF2), lambda b: (0, b)),
            pl.BlockSpec((None, height, step * TF2), lambda b: (index, 0, b)),
            fixed,
            fixed,
        ],
        out_specs=pl.BlockSpec((step * groups, height, LANES), lambda b: (b, 0, 0)),
        compiler_params=pltpu.CompilerParams(vmem_limit_bytes=24 * 2**20),
        cost_estimate=pl.CostEstimate(
            flops=6 * height * breadth * TF2, bytes_accessed=8 * height * breadth, transcendentals=0
        ),
    )(keeper, spectra, *split_table(table))


def kernel_rows(blocks, table):
    granules, height = blocks[0].shape[:2]
    groups = TF2 // LANES
    tiles = granules // groups
    number = len(blocks)
    step = tiles_at_once(tiles)
    fixed = pl.BlockSpec((TF2, TF2), lambda b: (0, 0))
    return pl.pallas_call(
        rows_kernel,
        grid=(tiles // step,),
        out_shape=jax.ShapeDtypeStruct((number, height, tiles * TF2), jnp.float32),
        in_specs=[pl.BlockSpec((step * groups, height, LANES), lambda b: (b, 0, 0))] * number
        + [fixed, fixed],
        out_specs=pl.BlockSpec((number, height, step * TF2), lambda b: (0, 0, b)),
        compiler_params=pltpu.CompilerParams(vmem_limit_bytes=24 * 2**20),
    )(*blocks, *split_table(table))


FOLD = F1 // 2
TILE_GROUPS = TF2 // LANES
BLOCK = 256
STRIP = 64
MESH_ID = pl.DeviceIdType.MESH


def folded_table():
    cosine, sine = trig(FOLD, F1, F1)
    sine[0] = np.where(np.arange(F1) % 2 == 0, 1.0, -1.0)
    return np.concatenate([cosine, sine])


def swapped(values):
    return pltpu.roll(values, LANES // 2, 1)


def rows_of(bins, table_high, table_low, out, chunk):
    count, height = bins.shape[:2]
    tiles = count // TILE_GROUPS
    parts = [
        jnp.concatenate([bins[tile * TILE_GROUPS + group] for group in range(TILE_GROUPS)], axis=1)
        for tile in range(tiles)
    ]
    values = product_of(jnp.concatenate(parts, axis=0), table_high[...], table_low[...])
    for tile in range(tiles):
        start = (chunk * tiles + tile) * TF2
        out[:, start : start + TF2] = values[tile * height : (tile + 1) * height]


def last_kernel(
    aligned_in, done, bins, last_high, last_low, correlation, aligned_out, fresh, sems
):
    width = done.shape[2]
    copies = [
        pltpu.make_async_copy(done, correlation.at[:, :, pl.ds(0, width)], sems.at[0]),
        pltpu.make_async_copy(aligned_in, aligned_out, sems.at[1]),
    ]
    for copy in copies:
        copy.start()
    for spectrum in range(bins.shape[0]):
        rows_of(bins.at[spectrum], last_high, last_low, fresh.at[spectrum], 0)
        copy = pltpu.make_async_copy(
            fresh.at[spectrum],
            correlation.at[spectrum, :, pl.ds(width, fresh.shape[2])],
            sems.at[2 + spectrum],
        )
        copy.start()
        copies.append(copy)
    for copy in copies:
        copy.wait()


def whole_kernel(
    edges_in,
    shifts_in,
    spectra,
    plane,
    row_high_in,
    row_low_in,
    col_high_in,
    col_low_in,
    back_high_in,
    back_low_in,
    last_high_in,
    last_low_in,
    aligned_out,
    correlation,
    bins_last,
    last_high,
    last_low,
    edges,
    shifts,
    row_high,
    row_low,
    col_high,
    col_low,
    back_high,
    back_low,
    padded,
    plane_rows,
    plane_sent,
    plane_got,
    sent,
    got,
    returned,
    bins,
    coefs,
    both,
    high,
    low,
    pair_high,
    pair_low,
    load_sem,
    halo_send,
    halo_got,
    plane_send_sem,
    plane_got_sem,
    swap_send_sem,
    swap_got_sem,
    spec_send_sem,
    spec_got_sem,
    back_send_sem,
    back_got_sem,
):
    number, height, breadth = spectra.shape
    count = lax.axis_size("rows")
    chunks = breadth // LANES // count
    per_chunk = count // TILE_GROUPS
    share = plane_rows.shape[0]
    me = lax.axis_index("rows")
    side = lax.axis_index("group")
    other = 1 - side
    middle = slice(LANES, LANES + breadth)

    def load(source, target, sem):
        copy = pltpu.make_async_copy(source, target, load_sem.at[sem])
        copy.start()
        return copy

    own = pl.ds(pl.multiple_of(side * share, share), share)
    loads = [
        load(plane.at[own], plane_rows, 0),
        load(row_high_in, row_high, 1),
        load(row_low_in, row_low, 2),
        load(spectra, padded.at[:, pl.ds(MAXS, height), pl.ds(LANES, breadth)], 3),
        load(col_high_in, col_high, 4),
        load(col_low_in, col_low, 5),
        load(back_high_in, back_high, 6),
        load(back_low_in, back_low, 7),
        load(last_high_in, last_high, 8),
        load(last_low_in, last_low, 9),
        load(edges_in, edges, 10),
        load(shifts_in, shifts, 11),
    ]

    barrier = pltpu.get_barrier_semaphore()

    def greet(step, carry):
        peer = lax.rem(me + step, count)
        pl.semaphore_signal(barrier, 1, device_id=(side, peer), device_id_type=MESH_ID)
        return carry

    lax.fori_loop(1, count, greet, 0)
    pl.semaphore_signal(barrier, 1, device_id=(other, me), device_id_type=MESH_ID)
    pl.semaphore_wait(barrier, count)

    def remote(source, target, send, got_sem, where):
        return pltpu.make_async_remote_copy(
            src_ref=source,
            dst_ref=target,
            send_sem=send,
            recv_sem=got_sem,
            device_id=where,
            device_id_type=MESH_ID,
        )

    def halo_down():
        return remote(
            spectra.at[:, pl.ds(height - MAXS, MAXS)],
            padded.at[:, pl.ds(0, MAXS), pl.ds(LANES, breadth)],
            halo_send.at[0],
            halo_got.at[0],
            (side, lax.rem(me + 1, count)),
        )

    def halo_up():
        return remote(
            spectra.at[:, pl.ds(0, MAXS)],
            padded.at[:, pl.ds(MAXS + height, MAXS), pl.ds(LANES, breadth)],
            halo_send.at[1],
            halo_got.at[1],
            (side, lax.rem(me + count - 1, count)),
        )

    @pl.when(me < count - 1)
    def _():
        halo_down().start()

    @pl.when(me > 0)
    def _():
        halo_up().start()

    def far_first(step, carry, start):
        half = lax.div(step + 1, 2)
        offset = count // 2 + half * (1 - 2 * lax.rem(step, 2))
        start(lax.rem(me + offset, count))
        return carry

    def to_all(start):
        lax.fori_loop(0, count - 1, lambda step, carry: far_first(step, carry, start), 0)

    loads[0].wait()
    loads[1].wait()
    loads[2].wait()
    for chunk in range(chunks):

        def bins_of(rows, table_high, table_low):
            return product_of(rows, table_high[...], table_low[...])

        tiles = [
            plane_rows[:, start : start + TF2]
            for start in range(chunk * per_chunk * TF2, (chunk + 1) * per_chunk * TF2, TF2)
        ]
        found = bins_of(jnp.concatenate(tiles, axis=0), row_high, row_low)
        for tile in range(per_chunk):
            for group in range(TILE_GROUPS):
                plane_sent[chunk, tile * TILE_GROUPS + group] = found[
                    tile * share : (tile + 1) * share, group * LANES : (group + 1) * LANES
                ]
        plane_got[chunk, me, own] = plane_sent[chunk, me]

        def send_plane(peer):
            remote(
                plane_sent.at[chunk, peer],
                plane_got.at[chunk, me, own],
                plane_send_sem.at[chunk],
                plane_got_sem.at[chunk],
                (side, peer),
            ).start()

        to_all(send_plane)

    loads[3].wait()
    loads[10].wait()
    loads[11].wait()
    column = lax.broadcasted_iota(jnp.int32, (1, TF2), 1)
    for chunk in range(chunks):

        def spectrum_bins(spectrum, carry):
            parts = []
            for tile in range(chunk * per_chunk, (chunk + 1) * per_chunk):
                inside = (column >= edges[0, tile]) & (column < TF2 - edges[1, tile])
                keeper = jnp.where(inside, 1.0, 0.0).astype(jnp.float32)
                lanes = slice(LANES + tile * TF2, LANES + (tile + 1) * TF2)
                parts.append(padded[spectrum, MAXS : MAXS + height, lanes] * keeper)
            found = product_of(jnp.concatenate(parts, axis=0), row_high[...], row_low[...])
            for tile in range(per_chunk):
                for group in range(TILE_GROUPS):
                    sent[chunk, spectrum, tile * TILE_GROUPS + group] = found[
                        tile * height : (tile + 1) * height, group * LANES : (group + 1) * LANES
                    ]
            got[chunk, spectrum, me] = sent[chunk, spectrum, me]

            def send_spectrum(peer):
                remote(
                    sent.at[chunk, spectrum, peer],
                    got.at[chunk, spectrum, me],
                    spec_send_sem.at[chunk, spectrum],
                    spec_got_sem.at[chunk, spectrum],
                    (side, peer),
                ).start()

            to_all(send_spectrum)
            return carry

        lax.fori_loop(0, number, spectrum_bins, 0)

    total = height + 2 * MAXS
    margin = jnp.zeros((number, total, LANES), jnp.float32)
    padded[:, :, :LANES] = margin
    padded[:, :, LANES + breadth :] = margin
    blank = jnp.zeros((number, MAXS, breadth), jnp.float32)

    @pl.when(me == 0)
    def _():
        padded[:, :MAXS, middle] = blank

    @pl.when(me == count - 1)
    def _():
        padded[:, MAXS + height :, middle] = blank

    @pl.when(me > 0)
    def _():
        halo_down().wait_recv()

    @pl.when(me < count - 1)
    def _():
        halo_up().wait_recv()

    window = TF2 + 2 * LANES
    for spectrum in range(number):

        @pl.loop(0, breadth // TF2)
        def _(tile):
            down = shifts[spectrum, 0, tile]
            right = shifts[spectrum, 1, tile]
            start = pl.multiple_of(tile * TF2, TF2)
            part = padded[spectrum, :, pl.ds(start, window)]
            part = pltpu.roll(part, lax.rem(right + window, window), 1)[:, LANES : LANES + TF2]
            part = pltpu.roll(part, lax.rem(down + total, total), 0)
            aligned_out[spectrum, :, pl.ds(start, TF2)] = part[MAXS : MAXS + height]

    def landed(buffer, sem):
        fifteen = buffer.at[pl.ds(0, count - 1)]
        pltpu.make_async_copy(fifteen, fifteen, sem).wait()

    def swap_plane(chunk):
        half = plane_got.at[chunk, :, own]
        return remote(
            half, half, swap_send_sem.at[chunk], swap_got_sem.at[chunk], (other, me)
        )

    for chunk in range(chunks):
        landed(plane_sent.at[chunk], plane_got_sem.at[chunk])
        swap_plane(chunk).start()

    def transform(width):
        @pl.loop(0, F1 // BLOCK)
        def _(step):
            rows = pl.ds(pl.multiple_of(step * BLOCK, BLOCK), BLOCK)
            both[rows, :width] = product_3(
                col_high, col_low, rows, high[:, :width], low[:, :width]
            )

    for load_index in range(4, 10):
        loads[load_index].wait()

    lane = lax.broadcasted_iota(jnp.int32, (STRIP, LANES), 1)
    is_real = lane < LANES // 2
    first_row = lax.broadcasted_iota(jnp.int32, (STRIP, LANES), 0) == 0
    alone = (lax.rem(lane, LANES // 2) == 0) & (lax.rem(me, TILE_GROUPS) == 0)

    def strips(body):
        @pl.loop(0, FOLD // STRIP)
        def _(step):
            start = pl.multiple_of(step * STRIP, STRIP)
            body(pl.ds(start, STRIP), pl.ds(FOLD + start, STRIP))

    zero = jnp.zeros((STRIP, LANES), jnp.float32)

    def plane_coefs(chunk):
        def body(top, bottom):
            c, s = both[top, :LANES], both[bottom, :LANES]
            sc, ss = swapped(c), swapped(s)
            c2, s2 = c + c, s + s
            coefs[chunk, 0, top, :] = jnp.where(alone | is_real, c2, sc + sc)
            coefs[chunk, 1, top, :] = jnp.where(alone, zero, jnp.where(is_real, sc + sc, -c2))
            coefs[chunk, 2, top, :] = jnp.where(alone | is_real, s2, ss + ss)
            coefs[chunk, 3, top, :] = jnp.where(alone, zero, jnp.where(is_real, ss + ss, -s2))

        strips(body)

    def store_pair(rows, lanes, values, high_ref, low_ref):
        high_ref[rows, lanes], low_ref[rows, lanes] = split(values)

    def pairs(chunk):
        for spectrum in range(number):
            lanes = slice(spectrum * LANES, (spectrum + 1) * LANES)

            def take(top, bottom):
                c, s = both[top, lanes], both[bottom, lanes]
                sc, ss = swapped(c), swapped(s)
                a, d = coefs[chunk, 0, top, :], coefs[chunk, 1, top, :]
                f, b = coefs[chunk, 2, top, :], coefs[chunk, 3, top, :]
                return c, s, sc, ss, a, d, f, b

            def body(top, bottom):
                c, s, sc, ss, a, d, f, b = take(top, bottom)
                store_pair(top, lanes, (c * a + sc * d) + (s * f + ss * b), pair_high, pair_low)
                store_pair(bottom, lanes, (s * a + ss * d) - (c * f + sc * b), pair_high, pair_low)

            strips(body)
            top, bottom = pl.ds(0, STRIP), pl.ds(FOLD, STRIP)
            c, s, sc, ss, a, d, f, b = take(top, bottom)
            zeroth = 0.5 * (c * a + sc * d)
            nyquist = 0.5 * (s * f + ss * b)
            first = (c * a + sc * d) + (s * f + ss * b)
            second = (s * a + ss * d) - (c * f + sc * b)
            store_pair(top, lanes, jnp.where(first_row, zeroth, first), pair_high, pair_low)
            store_pair(bottom, lanes, jnp.where(first_row, nyquist, second), pair_high, pair_low)

    def gather(block, lanes):
        @pl.loop(0, count)
        def _(source):
            rows = pl.ds(pl.multiple_of(source * height, height), height)
            high[rows, lanes], low[rows, lanes] = split(block[source])

    for chunk in range(chunks):
        swapped_half = plane_got.at[chunk, :, pl.ds(pl.multiple_of(other * share, share), share)]
        pltpu.make_async_copy(swapped_half, swapped_half, swap_got_sem.at[chunk]).wait()
        gather(plane_got.at[chunk], slice(0, LANES))
        transform(LANES)
        plane_coefs(chunk)

    for chunk in range(chunks):
        for spectrum in range(number):
            landed(got.at[chunk, spectrum], spec_got_sem.at[chunk, spectrum])
            gather(got.at[chunk, spectrum], slice(spectrum * LANES, (spectrum + 1) * LANES))
        transform(number * LANES)
        pairs(chunk)
        held = BLOCK // height
        target = bins.at[chunk] if chunk < chunks - 1 else bins_last

        def back(step, carry):
            place = lax.rem(lax.div(me, held) + count // held // 2 + step, count // held)
            rows = pl.ds(pl.multiple_of(place * BLOCK, BLOCK), BLOCK)
            values = product_3(back_high, back_low, rows, pair_high[...], pair_low[...])
            for spectrum in range(number):
                for part in range(held):
                    returned[chunk, spectrum, place * held + part] = values[
                        part * height : (part + 1) * height,
                        spectrum * LANES : (spectrum + 1) * LANES,
                    ]

            def send_back(index, inner):
                spectrum = lax.div(index, held)
                peer = place * held + lax.rem(index, held)

                @pl.when(peer != me)
                def _():
                    remote(
                        returned.at[chunk, spectrum, peer],
                        target.at[spectrum, me],
                        back_send_sem.at[chunk, spectrum],
                        back_got_sem.at[chunk, spectrum],
                        (side, peer),
                    ).start()

                return inner

            lax.fori_loop(0, number * held, send_back, 0)
            return carry

        lax.fori_loop(0, count // held, back, 0)
        for spectrum in range(number):
            target[spectrum, me] = returned[chunk, spectrum, me]

    for chunk in range(chunks - 1):
        for spectrum in range(number):
            landed(bins.at[chunk, spectrum], back_got_sem.at[chunk, spectrum])
            rows_of(bins.at[chunk, spectrum], last_high, last_low, correlation.at[spectrum], chunk)
    for spectrum in range(number):
        landed(bins_last.at[spectrum], back_got_sem.at[chunks - 1, spectrum])

    for chunk in range(chunks):
        landed(plane_sent.at[chunk], plane_send_sem.at[chunk])
        swap_plane(chunk).wait_send()
        for spectrum in range(number):
            landed(sent.at[chunk, spectrum], spec_send_sem.at[chunk, spectrum])
            landed(returned.at[chunk, spectrum], back_send_sem.at[chunk, spectrum])

    @pl.when(me < count - 1)
    def _():
        halo_down().wait_send()

    @pl.when(me > 0)
    def _():
        halo_up().wait_send()


def kernel_whole(spectra, plane, interval_edges, tile_shifts, forward, inverse):
    number, height, breadth = spectra.shape
    count = lax.axis_size("rows")
    share = height // lax.axis_size("group")
    chunks = breadth // LANES // count
    columns = folded_table()
    tables = (
        *split_table(forward),
        *split_table(columns),
        *split_table(np.ascontiguousarray(columns.T)),
        *split_table(inverse),
    )
    far = pl.BlockSpec(memory_space=pltpu.HBM)
    near = pl.BlockSpec(memory_space=pltpu.VMEM)
    breadths = (F1, number * LANES)
    blocks = (chunks, number, count, height, LANES)
    late = breadth // chunks
    held = (
        pltpu.VMEM(spectra.shape, jnp.float32),
        pltpu.VMEM((number, height, breadth - late), jnp.float32),
        pltpu.VMEM(blocks[1:], jnp.float32),
        pltpu.VMEM((TF2, TF2), jnp.bfloat16),
        pltpu.VMEM((TF2, TF2), jnp.bfloat16),
    )
    small = (interval_edges.T, tile_shifts.transpose(0, 2, 1))
    large = [
        pltpu.with_memory_space_constraint(value, pltpu.HBM)
        for value in (*small, spectra, plane, *map(jnp.asarray, tables))
    ]
    halfway = pl.pallas_call(
        whole_kernel,
        out_shape=held,
        in_specs=[far] * len(large),
        out_specs=(near,) * len(held),
        scratch_shapes=[pltpu.SMEM(value.shape, jnp.int32) for value in small]
        + [pltpu.VMEM(table.shape, jnp.bfloat16) for table in tables[:6]]
        + [
            pltpu.VMEM((number, height + 2 * MAXS, breadth + 2 * LANES), jnp.float32),
            pltpu.VMEM((share, breadth), jnp.float32),
            pltpu.VMEM((chunks, count, share, LANES), jnp.float32),
            pltpu.VMEM((chunks, count, height, LANES), jnp.float32),
            pltpu.VMEM(blocks, jnp.float32),
            pltpu.VMEM(blocks, jnp.float32),
            pltpu.VMEM(blocks, jnp.float32),
            pltpu.VMEM((chunks - 1,) + blocks[1:], jnp.float32),
            pltpu.VMEM((chunks, 4, FOLD, LANES), jnp.float32),
            pltpu.VMEM(breadths, jnp.float32),
            pltpu.VMEM(breadths, jnp.bfloat16),
            pltpu.VMEM(breadths, jnp.bfloat16),
            pltpu.VMEM(breadths, jnp.bfloat16),
            pltpu.VMEM(breadths, jnp.bfloat16),
            pltpu.SemaphoreType.DMA((12,)),
            pltpu.SemaphoreType.DMA((2,)),
            pltpu.SemaphoreType.DMA((2,)),
            pltpu.SemaphoreType.DMA((chunks,)),
            pltpu.SemaphoreType.DMA((chunks,)),
            pltpu.SemaphoreType.DMA((chunks,)),
            pltpu.SemaphoreType.DMA((chunks,)),
            pltpu.SemaphoreType.DMA((chunks, number)),
            pltpu.SemaphoreType.DMA((chunks, number)),
            pltpu.SemaphoreType.DMA((chunks, number)),
            pltpu.SemaphoreType.DMA((chunks, number)),
        ],
        compiler_params=pltpu.CompilerParams(
            collective_id=0, has_side_effects=True, vmem_limit_bytes=44 * 2**20
        ),
        cost_estimate=pl.CostEstimate(
            flops=2 * 3 * F1 * F1 * (2 * number + 2) * chunks * LANES,
            bytes_accessed=16 * spectra.size,
            transcendentals=0,
        ),
    )(*large)
    whole = jax.ShapeDtypeStruct(spectra.shape, jnp.float32)
    return pl.pallas_call(
        last_kernel,
        out_shape=(whole, whole),
        in_specs=[near] * len(held),
        out_specs=(pl.BlockSpec(memory_space=pltpu.HBM),) * 2,
        scratch_shapes=[
            pltpu.VMEM((number, height, late), jnp.float32),
            pltpu.SemaphoreType.DMA((2 + number,)),
        ],
        compiler_params=pltpu.CompilerParams(vmem_limit_bytes=16 * 2**20),
    )(*halfway)


def per_device(spectra, plane, interval_edges, tile_shifts):
    number, height, breadth = spectra.shape
    count = lax.axis_size("rows")
    tiles = breadth // TF2
    span = math.gcd(breadth // 2 // count, HALF)
    groups = HALF // span
    width = 2 * span
    local = tiles * groups // count
    forward, inverse = row_tables(span)

    point = jnp.arange(TF2, dtype=jnp.int32)[None, :]
    inside = (point >= interval_edges[:, 0:1]) & (point < TF2 - interval_edges[:, 1:2])
    keeper = jnp.where(inside, 1.0, 0.0).astype(jnp.float32).reshape(1, breadth)

    cohorts = lax.axis_size("group")
    share = height // cohorts
    whole_tiles = width == LANES and share % 16 == 0
    if whole_tiles and cohorts == 2 and height * count == F1 and count % groups == 0:
        tables = (forward.reshape(TF2, TF2), inverse.reshape(TF2, TF2))
        return kernel_whole(spectra, plane, interval_edges, tile_shifts, *tables)

    def to_columns(rows, index, kept, after=None):
        held = rows.shape[1]
        if whole_tiles:
            bins = kernel_bins(rows, index, kept, forward.reshape(TF2, TF2))
        else:
            blocks = (rows[index] * kept).reshape(held, tiles, TF2)
            table = forward.astype(np.float32)
            bins = jnp.einsum("rbn,njl->bjrl", blocks, table, precision=full)
        sent = bins.reshape(count, local, held, width)
        if after is not None:
            sent, _ = lax.optimization_barrier((sent, after))
        return lax.all_to_all(sent, "rows", split_axis=0, concat_axis=0, tiled=True)

    granule = lax.axis_index("rows") * local + jnp.arange(local, dtype=jnp.int32)
    packed = (granule % groups == 0)[:, None] & (jnp.arange(span) == 0)[None, :]
    own = lax.axis_index("group")
    plane_rows = lax.dynamic_slice_in_dim(plane, own * share, share, axis=0)
    mine = to_columns(plane_rows[None], 0, jnp.ones_like(keeper))
    if cohorts == 2:
        other = lax.ppermute(mine, "group", [(0, 1), (1, 0)])
        ordered = [jnp.where(own == 0, mine, other), jnp.where(own == 0, other, mine)]
        plane_columns = jnp.concatenate(ordered, axis=2)
    else:
        plane_columns = lax.all_gather(mine, "group", axis=2, tiled=True)
    plane_both = kernel_plane(plane_columns) if whole_tiles else None
    received = [to_columns(spectra, s, keeper, plane_both if s else None) for s in range(number)]
    aligned_spectra = aligned(spectra, tile_shifts)
    if whole_tiles:
        products = kernel_products(plane_both, received, packed)
    else:
        products = plain_products(plane_columns, received, packed)
    returned = [
        lax.all_to_all(block, "rows", split_axis=0, concat_axis=0, tiled=True)
        for block in products
    ]

    if whole_tiles:
        blocks = [block.reshape(tiles * groups, height, width) for block in returned]
        return (kernel_rows(blocks, inverse.reshape(TF2, TF2)), aligned_spectra)

    def to_rows(block):
        bins = block.reshape(tiles, groups, height, width)
        table = inverse.astype(np.float32)
        return jnp.einsum("bjrl,jln->rbn", bins, table, precision=full).reshape(height, breadth)

    correlation = jnp.stack([to_rows(block) for block in returned])
    return (correlation, aligned_spectra)


def solution(mesh):
    placed = (P("group", "rows", None), P("rows", None), P(), P("group", None, None))
    return jax.shard_map(
        per_device,
        mesh=mesh,
        in_specs=placed,
        out_specs=(P("group", "rows", None), P("group", "rows", None)),
        check_vma=False,
    )
```

```python
import math

import jax
import jax.numpy as jnp
import numpy as np
from jax import lax
from jax.experimental import pallas as pl
from jax.experimental.pallas import tpu as pltpu
from jax.sharding import PartitionSpec as P

F1 = 1024
TF2 = 512
HALF = TF2 // 2
MAXS = 8
LANES = 128

exact = lax.Precision.HIGH
full = lax.Precision.HIGHEST


def trig(rows, columns, modulus):
    angle = np.outer(np.arange(rows), np.arange(columns)) % modulus * (2.0 * math.pi / modulus)
    return np.cos(angle), np.sin(angle)


def column_table():
    return np.stack(trig(F1, F1, F1))


def row_tables(span):
    groups = HALF // span
    cosine, sine = trig(TF2, HALF, TF2)
    alternate = np.where(np.arange(TF2) % 2 == 0, 1.0, -1.0)
    forward_imag = -sine
    forward_imag[:, 0] = alternate
    forward = np.stack([cosine, forward_imag], axis=1)
    forward = forward.reshape(TF2, 2, groups, span).transpose(0, 2, 1, 3)
    forward = forward.reshape(TF2, groups, 2 * span)
    weights = np.where(np.arange(HALF) == 0, 1.0, 2.0)[None, :]
    inverse_imag = -2.0 * sine
    inverse_imag[:, 0] = alternate
    inverse = np.stack([weights * cosine, inverse_imag], axis=1)
    inverse = inverse.reshape(TF2, 2, groups, span).transpose(2, 1, 3, 0)
    inverse = inverse.reshape(groups, 2 * span, TF2) * float(F1 * TF2) ** (-1.5)
    return forward, inverse


def align_kernel(shifts, body, above, below, out, padded):
    spectrum = pl.program_id(0)
    height, breadth = body.shape[1:]
    total = height + 2 * MAXS
    margin = jnp.zeros((total, LANES), jnp.float32)
    padded[:, :LANES] = margin
    padded[:, LANES + breadth :] = margin
    padded[:MAXS, LANES : LANES + breadth] = above[0]
    padded[MAXS : MAXS + height, LANES : LANES + breadth] = body[0]
    padded[MAXS + height :, LANES : LANES + breadth] = below[0]
    window = TF2 + 2 * LANES
    for tile in range(breadth // TF2):
        down = shifts[spectrum, tile, 0]
        right = shifts[spectrum, tile, 1]
        part = padded[:, tile * TF2 : tile * TF2 + window]
        part = pltpu.roll(part, lax.rem(right + window, window), 1)[:, LANES : LANES + TF2]
        part = pltpu.roll(part, lax.rem(down + total, total), 0)
        out[0, :, tile * TF2 : (tile + 1) * TF2] = part[MAXS : MAXS + height]


def aligned(spectra, tile_shifts):
    number, height, breadth = spectra.shape
    count = lax.axis_size("rows")
    head = spectra[:, :MAXS]
    tail = spectra[:, height - MAXS :]
    above = lax.ppermute(tail, "rows", [(i, i + 1) for i in range(count - 1)])
    below = lax.ppermute(head, "rows", [(i + 1, i) for i in range(count - 1)])
    whole = pl.BlockSpec((1, height, breadth), lambda s: (s, 0, 0))
    edge = pl.BlockSpec((1, MAXS, breadth), lambda s: (s, 0, 0))
    return pl.pallas_call(
        align_kernel,
        grid=(number,),
        out_shape=jax.ShapeDtypeStruct(spectra.shape, jnp.float32),
        in_specs=[pl.BlockSpec(memory_space=pltpu.SMEM), whole, edge, edge],
        out_specs=whole,
        scratch_shapes=[pltpu.VMEM((height + 2 * MAXS, breadth + 2 * LANES), jnp.float32)],
        compiler_params=pltpu.CompilerParams(vmem_limit_bytes=24 * 2**20),
        cost_estimate=pl.CostEstimate(
            flops=20 * spectra.size, bytes_accessed=8 * spectra.size, transcendentals=0
        ),
    )(tile_shifts, spectra, above, below)


def plain_products(plane_columns, received, packed):
    count, local, height, width = plane_columns.shape
    span = width // 2
    columns = column_table().astype(np.float32)

    def halves(block):
        pencil = block.transpose(0, 2, 1, 3).reshape(F1, local * width)
        both = jnp.einsum("pkn,nl->pkl", columns, pencil, precision=exact)
        return both.reshape(2, F1, local, 2, span)

    def spectrum_of(both):
        cosine, sine = both[0], both[1]
        return cosine[:, :, 0] + sine[:, :, 1], cosine[:, :, 1] - sine[:, :, 0]

    plane_halves = halves(plane_columns)
    plane_real, plane_imag = spectrum_of(plane_halves)

    def back(block):
        both = halves(block)
        real, imag = spectrum_of(both)
        out_real = real * plane_real + imag * plane_imag
        out_imag = imag * plane_real - real * plane_imag
        cosine, sine = both[0], both[1]
        pc, ps = plane_halves[0], plane_halves[1]
        mask = packed[None, :, None, :]
        first = jnp.stack([out_real, out_imag], axis=2)
        second = jnp.stack([-out_imag, out_real], axis=2)
        first = jnp.where(mask, cosine * pc + sine * ps, first)
        second = jnp.where(mask, sine * pc - cosine * ps, second)
        pair = jnp.stack([first, second]).reshape(2, F1, local * width)
        rows = jnp.einsum("pkn,pnl->kl", columns, pair, precision=exact)
        return rows.reshape(count, height, local, width).transpose(0, 2, 1, 3)

    return [back(block) for block in received]


def split(values):
    high = values.astype(jnp.bfloat16)
    return high, (values - high.astype(jnp.float32)).astype(jnp.bfloat16)


def product_3(table_high, table_low, rows, high, low):
    def dot(a, b):
        return jnp.dot(a, b, preferred_element_type=jnp.float32)

    top = table_high[rows, :]
    return dot(top, high) + (dot(top, low) + dot(table_low[rows, :], high))


CHUNK = 256


def forward_halves(table_high, table_low, block, both, high, low):
    count, local, height, width = block.shape
    for source in range(count):
        for part in range(local):
            rows = slice(source * height, (source + 1) * height)
            lanes = slice(part * width, (part + 1) * width)
            high[rows, lanes], low[rows, lanes] = split(block[source, part])

    @pl.loop(0, 2 * F1 // CHUNK)
    def _(step):
        rows = pl.ds(pl.multiple_of(step * CHUNK, CHUNK), CHUNK)
        both[rows, :] = product_3(table_high, table_low, rows, high[...], low[...])


def product_kernel(
    table_high, table_low, block, plane_both, packed, out, both, high, low, pair_high, pair_low
):
    count, local, height, width = block.shape
    forward_halves(table_high, table_low, block, both, high, low)
    rows_per = 64
    lane = lax.broadcasted_iota(jnp.int32, (rows_per, width), 1)
    is_real = lane < width // 2
    sign = jnp.where(is_real, 1.0, -1.0).astype(jnp.float32)

    def swap(values):
        return pltpu.roll(values, width // 2, 1)

    @pl.loop(0, F1 // rows_per)
    def _(step):
        top = pl.ds(pl.multiple_of(step * rows_per, rows_per), rows_per)
        bottom = pl.ds(pl.multiple_of(F1 + step * rows_per, rows_per), rows_per)
        for part in range(local):
            lanes = slice(part * width, (part + 1) * width)
            c, s = both[top, lanes], both[bottom, lanes]
            pc, ps = plane_both[top, lanes], plane_both[bottom, lanes]
            value = c + sign * swap(s)
            plane_value = pc + sign * swap(ps)
            same = value * plane_value
            cross = swap(value) * plane_value
            product = jnp.where(is_real, same + swap(same), swap(cross) - cross)
            alone = packed[0:1, lanes] > 0.5
            first = jnp.where(alone, c * pc + s * ps, product)
            second = jnp.where(alone, s * pc - c * ps, -sign * swap(product))
            pair_high[top, lanes], pair_low[top, lanes] = split(first)
            pair_high[bottom, lanes], pair_low[bottom, lanes] = split(second)

    per_step = CHUNK // height

    @pl.loop(0, F1 // CHUNK)
    def _(step):
        total = jnp.zeros((CHUNK, local * width), jnp.float32)
        for side in range(2):
            rows = pl.ds(pl.multiple_of(side * F1 + step * CHUNK, CHUNK), CHUNK)
            own = slice(side * F1, (side + 1) * F1)
            total += product_3(table_high, table_low, rows, pair_high[own], pair_low[own])
        for place in range(per_step):
            for part in range(local):
                out[step * per_step + place, part] = total[
                    place * height : (place + 1) * height, part * width : (part + 1) * width
                ]


def column_parts():
    return split_table(column_table().reshape(2 * F1, F1))


def kernel_plane(plane_columns):
    breadth = plane_columns.shape[1] * plane_columns.shape[3]
    space = pl.BlockSpec(memory_space=pltpu.VMEM)
    return pl.pallas_call(
        forward_halves,
        out_shape=jax.ShapeDtypeStruct((2 * F1, breadth), jnp.float32),
        in_specs=[space] * 3,
        out_specs=space,
        scratch_shapes=[pltpu.VMEM((F1, breadth), jnp.bfloat16)] * 2,
        compiler_params=pltpu.CompilerParams(vmem_limit_bytes=44 * 2**20),
        cost_estimate=pl.CostEstimate(
            flops=12 * F1 * F1 * breadth, bytes_accessed=8 * F1 * F1, transcendentals=0
        ),
    )(*column_parts(), plane_columns)


def kernel_products(plane_both, received, packed):
    breadth = plane_both.shape[1]
    lanes = jnp.stack([packed, packed], axis=1).reshape(1, breadth).astype(jnp.float32)
    space = pl.BlockSpec(memory_space=pltpu.VMEM)
    halves_shape = (2 * F1, breadth)
    call = pl.pallas_call(
        product_kernel,
        out_shape=jax.ShapeDtypeStruct(received[0].shape, jnp.float32),
        in_specs=[space] * 5,
        out_specs=space,
        scratch_shapes=[pltpu.VMEM(halves_shape, jnp.float32)]
        + [pltpu.VMEM((F1, breadth), jnp.bfloat16)] * 2
        + [pltpu.VMEM(halves_shape, jnp.bfloat16)] * 2,
        compiler_params=pltpu.CompilerParams(vmem_limit_bytes=44 * 2**20),
        cost_estimate=pl.CostEstimate(
            flops=24 * F1 * F1 * breadth, bytes_accessed=8 * F1 * F1, transcendentals=0
        ),
    )
    return [call(*column_parts(), block, plane_both, lanes) for block in received]


def product_of(values, table_high, table_low):
    high, low = split(values)

    def dot(a, b):
        return jnp.dot(a, b, preferred_element_type=jnp.float32)

    count = values.shape[0]
    both = dot(jnp.concatenate([high, low], axis=0), table_high)
    return both[:count] + (both[count:] + dot(high, table_low))


def bins_kernel(keeper, rows, table_high, table_low, out):
    height, breadth = rows.shape
    groups = TF2 // LANES
    values = rows[...] * keeper[...]
    tiles = [values[:, start : start + TF2] for start in range(0, breadth, TF2)]
    bins = product_of(jnp.concatenate(tiles, axis=0), table_high[...], table_low[...])
    for tile in range(len(tiles)):
        for group in range(groups):
            out[tile * groups + group] = bins[
                tile * height : (tile + 1) * height, group * LANES : (group + 1) * LANES
            ]


def rows_kernel(*refs):
    blocks, (table_high, table_low, out) = refs[:-3], refs[-3:]
    granules, height = blocks[0].shape[:2]
    groups = TF2 // LANES
    places = [(s, t) for s in range(len(blocks)) for t in range(granules // groups)]
    parts = [
        jnp.concatenate([blocks[s][t * groups + group] for group in range(groups)], axis=1)
        for s, t in places
    ]
    rows = product_of(jnp.concatenate(parts, axis=0), table_high[...], table_low[...])
    for place, (s, t) in enumerate(places):
        out[s, :, t * TF2 : (t + 1) * TF2] = rows[place * height : (place + 1) * height]


def tiles_at_once(tiles):
    return 3 if tiles % 3 == 0 else 2 if tiles % 2 == 0 else 1


def split_table(table):
    high = table.astype(jnp.bfloat16)
    return high, (table - high.astype(np.float64)).astype(jnp.bfloat16)


def kernel_bins(spectra, index, keeper, table):
    height, breadth = spectra.shape[1:]
    tiles, groups = breadth // TF2, TF2 // LANES
    step = tiles_at_once(tiles)
    fixed = pl.BlockSpec((TF2, TF2), lambda b: (0, 0))
    return pl.pallas_call(
        bins_kernel,
        grid=(tiles // step,),
        out_shape=jax.ShapeDtypeStruct((tiles * groups, height, LANES), jnp.float32),
        in_specs=[
            pl.BlockSpec((1, step * TF2), lambda b: (0, b)),
            pl.BlockSpec((None, height, step * TF2), lambda b: (index, 0, b)),
            fixed,
            fixed,
        ],
        out_specs=pl.BlockSpec((step * groups, height, LANES), lambda b: (b, 0, 0)),
        compiler_params=pltpu.CompilerParams(vmem_limit_bytes=24 * 2**20),
        cost_estimate=pl.CostEstimate(
            flops=6 * height * breadth * TF2, bytes_accessed=8 * height * breadth, transcendentals=0
        ),
    )(keeper, spectra, *split_table(table))


def kernel_rows(blocks, table):
    granules, height = blocks[0].shape[:2]
    groups = TF2 // LANES
    tiles = granules // groups
    number = len(blocks)
    step = tiles_at_once(tiles)
    fixed = pl.BlockSpec((TF2, TF2), lambda b: (0, 0))
    return pl.pallas_call(
        rows_kernel,
        grid=(tiles // step,),
        out_shape=jax.ShapeDtypeStruct((number, height, tiles * TF2), jnp.float32),
        in_specs=[pl.BlockSpec((step * groups, height, LANES), lambda b: (b, 0, 0))] * number
        + [fixed, fixed],
        out_specs=pl.BlockSpec((number, height, step * TF2), lambda b: (0, 0, b)),
        compiler_params=pltpu.CompilerParams(vmem_limit_bytes=24 * 2**20),
    )(*blocks, *split_table(table))


FOLD = F1 // 2
TILE_GROUPS = TF2 // LANES
BLOCK = 256
STRIP = 64
QUAD = 4
MESH_ID = pl.DeviceIdType.MESH


def folded_table():
    cosine, sine = trig(FOLD, F1, F1)
    sine[0] = np.where(np.arange(F1) % 2 == 0, 1.0, -1.0)
    return np.concatenate([cosine, sine])


def swapped(values):
    return pltpu.roll(values, LANES // 2, 1)


def rows_of(bins, table_high, table_low, out, chunk):
    count, height = bins.shape[:2]
    tiles = count // TILE_GROUPS
    parts = [
        jnp.concatenate([bins[tile * TILE_GROUPS + group] for group in range(TILE_GROUPS)], axis=1)
        for tile in range(tiles)
    ]
    values = product_of(jnp.concatenate(parts, axis=0), table_high[...], table_low[...])
    for tile in range(tiles):
        start = (chunk * tiles + tile) * TF2
        out[:, start : start + TF2] = values[tile * height : (tile + 1) * height]


def last_kernel(
    aligned_in, done, bins, ready, last_high, last_low, correlation, aligned_out, fresh, sems
):
    width, late, last = done.shape[2], fresh.shape[1], bins.shape[0] - 1
    copies = [
        pltpu.make_async_copy(aligned_in, aligned_out, sems.at[0]),
        pltpu.make_async_copy(done, correlation.at[:, :, pl.ds(0, width)], sems.at[1]),
        pltpu.make_async_copy(
            ready, correlation.at[pl.ds(0, last), :, pl.ds(width, late)], sems.at[2]
        ),
        pltpu.make_async_copy(fresh, correlation.at[last, :, pl.ds(width, late)], sems.at[3]),
    ]
    for copy in copies[:3]:
        copy.start()
    rows_of(bins.at[last], last_high, last_low, fresh, 0)
    copies[3].start()
    for copy in copies:
        copy.wait()


def whole_kernel(
    edges_in,
    shifts_in,
    spectra,
    plane,
    row_high_in,
    row_low_in,
    col_high_in,
    col_low_in,
    back_high_in,
    back_low_in,
    last_high_in,
    last_low_in,
    aligned_out,
    correlation,
    bins_last,
    fresh,
    last_high,
    last_low,
    edges,
    shifts,
    row_high,
    row_low,
    col_high,
    col_low,
    back_high,
    back_low,
    padded,
    plane_rows,
    plane_sent,
    plane_got,
    sent,
    got,
    returned,
    bins,
    coefs,
    both,
    high,
    low,
    pair_high,
    pair_low,
    load_sem,
    halo_send,
    halo_got,
    detour,
    detour_send,
    detour_got,
    plane_send_sem,
    plane_got_sem,
    swap_send_sem,
    swap_got_sem,
    spec_send_sem,
    spec_got_sem,
    back_send_sem,
    back_got_sem,
):
    number, height, breadth = spectra.shape
    count = lax.axis_size("rows")
    chunks = breadth // LANES // count
    per_chunk = count // TILE_GROUPS
    share = plane_rows.shape[0]
    me = lax.axis_index("rows")
    side = lax.axis_index("group")
    other = 1 - side
    middle = slice(LANES, LANES + breadth)

    barrier = pltpu.get_barrier_semaphore()

    def greet(step, carry):
        peer = lax.rem(me + step, count)
        pl.semaphore_signal(barrier, 1, device_id=(side, peer), device_id_type=MESH_ID)
        return carry

    lax.fori_loop(1, count, greet, 0)
    pl.semaphore_signal(barrier, 1, device_id=(other, me), device_id_type=MESH_ID)

    def load(source, target, sem):
        copy = pltpu.make_async_copy(source, target, load_sem.at[sem])
        copy.start()
        return copy

    own = pl.ds(pl.multiple_of(side * share, share), share)
    loads = [
        load(plane.at[own], plane_rows, 0),
        load(row_high_in, row_high, 1),
        load(row_low_in, row_low, 2),
        load(spectra, padded.at[:, pl.ds(MAXS, height), pl.ds(LANES, breadth)], 3),
        load(col_high_in, col_high, 4),
        load(col_low_in, col_low, 5),
        load(back_high_in, back_high, 6),
        load(back_low_in, back_low, 7),
        load(last_high_in, last_high, 8),
        load(last_low_in, last_low, 9),
        load(edges_in, edges, 10),
        load(shifts_in, shifts, 11),
    ]

    def remote(source, target, send, got_sem, where):
        return pltpu.make_async_remote_copy(
            src_ref=source,
            dst_ref=target,
            send_sem=send,
            recv_sem=got_sem,
            device_id=where,
            device_id_type=MESH_ID,
        )

    last = number - 1
    middle_low, middle_high = count // 2 - 1, count // 2
    senders, takers = (middle_low, middle_high), (middle_high, middle_low)
    detours = (middle_low - 2, middle_high + 2)
    outside = pl.ds(0, MAXS), pl.ds(MAXS + height, MAXS)
    inside_rows = pl.ds(height - MAXS, MAXS), pl.ds(0, MAXS)
    has_next = (me < count - 1, me > 0)
    has_previous = (me > 0, me < count - 1)

    def halo(way, which):
        kept = pl.ds(0, last) if which == 0 else pl.ds(last, 1)
        peer = lax.rem(me + (1, count - 1)[way], count)
        return remote(
            spectra.at[kept, inside_rows[way]],
            padded.at[kept, outside[way], pl.ds(LANES, breadth)],
            halo_send.at[way, which],
            halo_got.at[way, which],
            (side, peer),
        )

    def detour_out(way):
        return remote(
            spectra.at[pl.ds(last, 1), inside_rows[way]],
            detour.at[way],
            halo_send.at[way, 1],
            detour_got.at[way],
            (side, detours[way]),
        )

    def detour_on(way):
        return remote(
            detour.at[way],
            padded.at[pl.ds(last, 1), outside[way], pl.ds(LANES, breadth)],
            detour_send.at[way],
            halo_got.at[way, 1],
            (side, takers[way]),
        )

    def send_halos():
        for way in range(2):
            pl.when(has_next[way])(lambda: halo(way, 0).start())
            pl.when(has_next[way] & (me != senders[way]))(lambda: halo(way, 1).start())
            pl.when(me == senders[way])(lambda: detour_out(way).start())

    def pass_halos():
        for way in range(2):

            @pl.when(me == detours[way])
            def _():
                detour_out(way).wait_recv()
                detour_on(way).start()

    def take_halos():
        for way in range(2):
            for which in range(2):
                pl.when(has_previous[way])(lambda: halo(way, which).wait_recv())

    def finish_halos():
        for way in range(2):
            for which in range(2):
                pl.when(has_next[way])(lambda: halo(way, which).wait_send())
            pl.when(me == detours[way])(lambda: detour_on(way).wait_send())

    def to_all(start):
        def one(step, carry):
            half = lax.div(step + 1, 2)
            offset = count // 2 + half * (1 - 2 * lax.rem(step, 2))
            start(lax.rem(me + offset, count))
            return carry

        lax.fori_loop(0, count - 1, one, 0)

    def to_all_last(start):
        quad, place = lax.div(me, QUAD), lax.rem(me, QUAD)
        across = 2 * (1 - lax.div(quad, 2))
        for target in (across, across + 1, quad + 1 - 2 * lax.rem(quad, 2)):
            for turn in range(QUAD):
                start(target * QUAD + lax.rem(place + turn, QUAD))
        for turn in range(1, QUAD):
            start(quad * QUAD + lax.rem(place + turn, QUAD))

    column = lax.broadcasted_iota(jnp.int32, (1, TF2), 1)
    total = height + 2 * MAXS
    window = TF2 + 2 * LANES

    def landed(buffer, sem):
        fifteen = buffer.at[pl.ds(0, count - 1)]
        pltpu.make_async_copy(fifteen, fifteen, sem).wait()

    def swap_plane(chunk):
        half = plane_got.at[chunk, :, own]
        return remote(
            half, half, swap_send_sem.at[chunk], swap_got_sem.at[chunk], (other, me)
        )

    def transform(width):
        @pl.loop(0, F1 // BLOCK)
        def _(step):
            rows = pl.ds(pl.multiple_of(step * BLOCK, BLOCK), BLOCK)
            both[rows, :width] = product_3(
                col_high, col_low, rows, high[:, :width], low[:, :width]
            )

    lane = lax.broadcasted_iota(jnp.int32, (STRIP, LANES), 1)
    is_real = lane < LANES // 2
    first_row = lax.broadcasted_iota(jnp.int32, (STRIP, LANES), 0) == 0
    alone = (lax.rem(lane, LANES // 2) == 0) & (lax.rem(me, TILE_GROUPS) == 0)

    def strips(body):
        @pl.loop(0, FOLD // STRIP)
        def _(step):
            start = pl.multiple_of(step * STRIP, STRIP)
            body(pl.ds(start, STRIP), pl.ds(FOLD + start, STRIP))

    zero = jnp.zeros((STRIP, LANES), jnp.float32)

    def plane_coefs(chunk):
        def body(top, bottom):
            c, s = both[top, :LANES], both[bottom, :LANES]
            sc, ss = swapped(c), swapped(s)
            c2, s2 = c + c, s + s
            coefs[chunk, 0, top, :] = jnp.where(alone | is_real, c2, sc + sc)
            coefs[chunk, 1, top, :] = jnp.where(alone, zero, jnp.where(is_real, sc + sc, -c2))
            coefs[chunk, 2, top, :] = jnp.where(alone | is_real, s2, ss + ss)
            coefs[chunk, 3, top, :] = jnp.where(alone, zero, jnp.where(is_real, ss + ss, -s2))

        strips(body)

    def store_pair(rows, lanes, values, high_ref, low_ref):
        high_ref[rows, lanes], low_ref[rows, lanes] = split(values)

    def pairs(chunk):
        for spectrum in range(number):
            lanes = slice(spectrum * LANES, (spectrum + 1) * LANES)

            def take(top, bottom):
                c, s = both[top, lanes], both[bottom, lanes]
                sc, ss = swapped(c), swapped(s)
                a, d = coefs[chunk, 0, top, :], coefs[chunk, 1, top, :]
                f, b = coefs[chunk, 2, top, :], coefs[chunk, 3, top, :]
                return c, s, sc, ss, a, d, f, b

            def body(top, bottom):
                c, s, sc, ss, a, d, f, b = take(top, bottom)
                store_pair(top, lanes, (c * a + sc * d) + (s * f + ss * b), pair_high, pair_low)
                store_pair(bottom, lanes, (s * a + ss * d) - (c * f + sc * b), pair_high, pair_low)

            strips(body)
            top, bottom = pl.ds(0, STRIP), pl.ds(FOLD, STRIP)
            c, s, sc, ss, a, d, f, b = take(top, bottom)
            zeroth = 0.5 * (c * a + sc * d)
            nyquist = 0.5 * (s * f + ss * b)
            first = (c * a + sc * d) + (s * f + ss * b)
            second = (s * a + ss * d) - (c * f + sc * b)
            store_pair(top, lanes, jnp.where(first_row, zeroth, first), pair_high, pair_low)
            store_pair(bottom, lanes, jnp.where(first_row, nyquist, second), pair_high, pair_low)

    def gather(block, lanes):
        @pl.loop(0, count)
        def _(source):
            rows = pl.ds(pl.multiple_of(source * height, height), height)
            high[rows, lanes], low[rows, lanes] = split(block[source])
    held = BLOCK // height

    def send_plane_bins(chunk):
        tiles = [
            plane_rows[:, start : start + TF2]
            for start in range(chunk * per_chunk * TF2, (chunk + 1) * per_chunk * TF2, TF2)
        ]
        found = product_of(jnp.concatenate(tiles, axis=0), row_high[...], row_low[...])
        for tile in range(per_chunk):
            for group in range(TILE_GROUPS):
                plane_sent[chunk, tile * TILE_GROUPS + group] = found[
                    tile * share : (tile + 1) * share, group * LANES : (group + 1) * LANES
                ]
        plane_got[chunk, me, own] = plane_sent[chunk, me]

        if chunk == 0:
            pl.semaphore_wait(barrier, count)

        def send_plane(peer):
            remote(
                plane_sent.at[chunk, peer],
                plane_got.at[chunk, me, own],
                plane_send_sem.at[chunk],
                plane_got_sem.at[chunk],
                (side, peer),
            ).start()

        to_all(send_plane)

    def send_spectra_bins(chunk):
        def spectrum_bins(spectrum, carry):
            parts = []
            for tile in range(chunk * per_chunk, (chunk + 1) * per_chunk):
                inside = (column >= edges[0, tile]) & (column < TF2 - edges[1, tile])
                keeper = jnp.where(inside, 1.0, 0.0).astype(jnp.float32)
                lanes = slice(LANES + tile * TF2, LANES + (tile + 1) * TF2)
                parts.append(padded[spectrum, MAXS : MAXS + height, lanes] * keeper)
            found = product_of(jnp.concatenate(parts, axis=0), row_high[...], row_low[...])
            for tile in range(per_chunk):
                for group in range(TILE_GROUPS):
                    sent[chunk, spectrum, tile * TILE_GROUPS + group] = found[
                        tile * height : (tile + 1) * height, group * LANES : (group + 1) * LANES
                    ]
            got[chunk, spectrum, me] = sent[chunk, spectrum, me]

            def send_spectrum(peer):
                remote(
                    sent.at[chunk, spectrum, peer],
                    got.at[chunk, spectrum, me],
                    spec_send_sem.at[chunk, spectrum],
                    spec_got_sem.at[chunk, spectrum],
                    (side, peer),
                ).start()

            to_all(send_spectrum)
            return carry

        lax.fori_loop(0, number, spectrum_bins, 0)

    def align():
        margin = jnp.zeros((number, total, LANES), jnp.float32)
        padded[:, :, :LANES] = margin
        padded[:, :, LANES + breadth :] = margin
        blank = jnp.zeros((number, MAXS, breadth), jnp.float32)

        @pl.when(me == 0)
        def _():
            padded[:, :MAXS, middle] = blank

        @pl.when(me == count - 1)
        def _():
            padded[:, MAXS + height :, middle] = blank


        for spectrum in range(number):

            @pl.loop(0, breadth // TF2)
            def _(tile):
                down = shifts[spectrum, 0, tile]
                right = shifts[spectrum, 1, tile]
                start = pl.multiple_of(tile * TF2, TF2)
                part = padded[spectrum, :, pl.ds(start, window)]
                part = pltpu.roll(part, lax.rem(right + window, window), 1)[:, LANES : LANES + TF2]
                part = pltpu.roll(part, lax.rem(down + total, total), 0)
                aligned_out[spectrum, :, pl.ds(start, TF2)] = part[MAXS : MAXS + height]

    def exchange_plane(chunk):
        landed(plane_sent.at[chunk], plane_got_sem.at[chunk])
        swap_plane(chunk).start()

    def transform_plane(chunk):
        swapped_half = plane_got.at[chunk, :, pl.ds(pl.multiple_of(other * share, share), share)]
        pltpu.make_async_copy(swapped_half, swapped_half, swap_got_sem.at[chunk]).wait()
        gather(plane_got.at[chunk], slice(0, LANES))
        transform(LANES)
        plane_coefs(chunk)

    def multiply(chunk):
        for spectrum in range(number):
            landed(got.at[chunk, spectrum], spec_got_sem.at[chunk, spectrum])
            gather(got.at[chunk, spectrum], slice(spectrum * LANES, (spectrum + 1) * LANES))
        transform(number * LANES)
        pairs(chunk)
        target = bins.at[chunk] if chunk < chunks - 1 else bins_last

        def back(step, carry):
            place = step
            rows = pl.ds(pl.multiple_of(place * BLOCK, BLOCK), BLOCK)
            values = product_3(back_high, back_low, rows, pair_high[...], pair_low[...])
            for spectrum in range(number):
                for part in range(held):
                    returned[chunk, spectrum, place * held + part] = values[
                        part * height : (part + 1) * height,
                        spectrum * LANES : (spectrum + 1) * LANES,
                    ]

            return carry

        lax.fori_loop(0, count // held, back, 0)
        for spectrum in range(number):

            def send_back(peer):
                remote(
                    returned.at[chunk, spectrum, peer],
                    target.at[spectrum, me],
                    back_send_sem.at[chunk, spectrum],
                    back_got_sem.at[chunk, spectrum],
                    (side, peer),
                ).start()

            (to_all if chunk < chunks - 1 else to_all_last)(send_back)
            target[spectrum, me] = returned[chunk, spectrum, me]

    def finish_rows(chunk):
        for spectrum in range(number):
            landed(bins.at[chunk, spectrum], back_got_sem.at[chunk, spectrum])
            rows_of(bins.at[chunk, spectrum], last_high, last_low, correlation.at[spectrum], chunk)

    for load_index in (0, 1, 2):
        loads[load_index].wait()
    for chunk in range(chunks):
        send_plane_bins(chunk)
    for load_index in (3, 10, 11):
        loads[load_index].wait()
    send_spectra_bins(0)
    for chunk in range(chunks):
        exchange_plane(chunk)
    for chunk in range(1, chunks):
        send_spectra_bins(chunk)
        if chunk == 1:
            send_halos()
    for load_index in range(4, 10):
        loads[load_index].wait()
    for chunk in range(chunks):
        transform_plane(chunk)
    pass_halos()
    for chunk in range(chunks):
        multiply(chunk)
    take_halos()
    align()
    for chunk in range(chunks - 1):
        finish_rows(chunk)
    for spectrum in range(number):
        landed(bins_last.at[spectrum], back_got_sem.at[chunks - 1, spectrum])
        if spectrum < number - 1:
            rows_of(bins_last.at[spectrum], last_high, last_low, fresh.at[spectrum], 0)

    for chunk in range(chunks):
        landed(plane_sent.at[chunk], plane_send_sem.at[chunk])
        swap_plane(chunk).wait_send()
        for spectrum in range(number):
            landed(sent.at[chunk, spectrum], spec_send_sem.at[chunk, spectrum])
            landed(returned.at[chunk, spectrum], back_send_sem.at[chunk, spectrum])

    finish_halos()

def kernel_whole(spectra, plane, interval_edges, tile_shifts, forward, inverse):
    number, height, breadth = spectra.shape
    count = lax.axis_size("rows")
    share = height // lax.axis_size("group")
    chunks = breadth // LANES // count
    columns = folded_table()
    tables = (
        *split_table(forward),
        *split_table(columns),
        *split_table(np.ascontiguousarray(columns.T)),
        *split_table(inverse),
    )
    far = pl.BlockSpec(memory_space=pltpu.HBM)
    near = pl.BlockSpec(memory_space=pltpu.VMEM)
    breadths = (F1, number * LANES)
    blocks = (chunks, number, count, height, LANES)
    late = breadth // chunks
    held = (
        pltpu.VMEM(spectra.shape, jnp.float32),
        pltpu.VMEM((number, height, breadth - late), jnp.float32),
        pltpu.VMEM(blocks[1:], jnp.float32),
        pltpu.VMEM((number - 1, height, late), jnp.float32),
        pltpu.VMEM((TF2, TF2), jnp.bfloat16),
        pltpu.VMEM((TF2, TF2), jnp.bfloat16),
    )
    small = (interval_edges.T, tile_shifts.transpose(0, 2, 1))
    large = [
        pltpu.with_memory_space_constraint(value, pltpu.HBM)
        for value in (*small, spectra, plane, *map(jnp.asarray, tables))
    ]
    halfway = pl.pallas_call(
        whole_kernel,
        out_shape=held,
        in_specs=[far] * len(large),
        out_specs=(near,) * len(held),
        scratch_shapes=[pltpu.SMEM(value.shape, jnp.int32) for value in small]
        + [pltpu.VMEM(table.shape, jnp.bfloat16) for table in tables[:6]]
        + [
            pltpu.VMEM((number, height + 2 * MAXS, breadth + 2 * LANES), jnp.float32),
            pltpu.VMEM((share, breadth), jnp.float32),
            pltpu.VMEM((chunks, count, share, LANES), jnp.float32),
            pltpu.VMEM((chunks, count, height, LANES), jnp.float32),
            pltpu.VMEM(blocks, jnp.float32),
            pltpu.VMEM(blocks, jnp.float32),
            pltpu.VMEM(blocks, jnp.float32),
            pltpu.VMEM((chunks - 1,) + blocks[1:], jnp.float32),
            pltpu.VMEM((chunks, 4, FOLD, LANES), jnp.float32),
            pltpu.VMEM(breadths, jnp.float32),
            pltpu.VMEM(breadths, jnp.bfloat16),
            pltpu.VMEM(breadths, jnp.bfloat16),
            pltpu.VMEM(breadths, jnp.bfloat16),
            pltpu.VMEM(breadths, jnp.bfloat16),
            pltpu.SemaphoreType.DMA((12,)),
            pltpu.SemaphoreType.DMA((2, 2)),
            pltpu.SemaphoreType.DMA((2, 2)),
            pltpu.VMEM((2, 1, MAXS, breadth), jnp.float32),
            pltpu.SemaphoreType.DMA((2,)),
            pltpu.SemaphoreType.DMA((2,)),
            pltpu.SemaphoreType.DMA((chunks,)),
            pltpu.SemaphoreType.DMA((chunks,)),
            pltpu.SemaphoreType.DMA((chunks,)),
            pltpu.SemaphoreType.DMA((chunks,)),
            pltpu.SemaphoreType.DMA((chunks, number)),
            pltpu.SemaphoreType.DMA((chunks, number)),
            pltpu.SemaphoreType.DMA((chunks, number)),
            pltpu.SemaphoreType.DMA((chunks, number)),
        ],
        compiler_params=pltpu.CompilerParams(
            collective_id=0, has_side_effects=True, vmem_limit_bytes=44 * 2**20
        ),
        cost_estimate=pl.CostEstimate(
            flops=2 * 3 * F1 * F1 * (2 * number + 2) * chunks * LANES,
            bytes_accessed=16 * spectra.size,
            transcendentals=0,
        ),
    )(*large)
    whole = jax.ShapeDtypeStruct(spectra.shape, jnp.float32)
    return pl.pallas_call(
        last_kernel,
        out_shape=(whole, whole),
        in_specs=[near] * len(held),
        out_specs=(pl.BlockSpec(memory_space=pltpu.HBM),) * 2,
        scratch_shapes=[
            pltpu.VMEM((height, late), jnp.float32),
            pltpu.SemaphoreType.DMA((4,)),
        ],
        compiler_params=pltpu.CompilerParams(vmem_limit_bytes=16 * 2**20),
    )(*halfway)


def per_device(spectra, plane, interval_edges, tile_shifts):
    number, height, breadth = spectra.shape
    count = lax.axis_size("rows")
    tiles = breadth // TF2
    span = math.gcd(breadth // 2 // count, HALF)
    groups = HALF // span
    width = 2 * span
    local = tiles * groups // count
    forward, inverse = row_tables(span)

    point = jnp.arange(TF2, dtype=jnp.int32)[None, :]
    inside = (point >= interval_edges[:, 0:1]) & (point < TF2 - interval_edges[:, 1:2])
    keeper = jnp.where(inside, 1.0, 0.0).astype(jnp.float32).reshape(1, breadth)

    cohorts = lax.axis_size("group")
    share = height // cohorts
    whole_tiles = width == LANES and share % 16 == 0
    if whole_tiles and cohorts == 2 and height * count == F1 and count == QUAD * QUAD and number > 1:
        tables = (forward.reshape(TF2, TF2), inverse.reshape(TF2, TF2))
        return kernel_whole(spectra, plane, interval_edges, tile_shifts, *tables)

    def to_columns(rows, index, kept, after=None):
        held = rows.shape[1]
        if whole_tiles:
            bins = kernel_bins(rows, index, kept, forward.reshape(TF2, TF2))
        else:
            blocks = (rows[index] * kept).reshape(held, tiles, TF2)
            table = forward.astype(np.float32)
            bins = jnp.einsum("rbn,njl->bjrl", blocks, table, precision=full)
        sent = bins.reshape(count, local, held, width)
        if after is not None:
            sent, _ = lax.optimization_barrier((sent, after))
        return lax.all_to_all(sent, "rows", split_axis=0, concat_axis=0, tiled=True)

    granule = lax.axis_index("rows") * local + jnp.arange(local, dtype=jnp.int32)
    packed = (granule % groups == 0)[:, None] & (jnp.arange(span) == 0)[None, :]
    own = lax.axis_index("group")
    plane_rows = lax.dynamic_slice_in_dim(plane, own * share, share, axis=0)
    mine = to_columns(plane_rows[None], 0, jnp.ones_like(keeper))
    if cohorts == 2:
        other = lax.ppermute(mine, "group", [(0, 1), (1, 0)])
        ordered = [jnp.where(own == 0, mine, other), jnp.where(own == 0, other, mine)]
        plane_columns = jnp.concatenate(ordered, axis=2)
    else:
        plane_columns = lax.all_gather(mine, "group", axis=2, tiled=True)
    plane_both = kernel_plane(plane_columns) if whole_tiles else None
    received = [to_columns(spectra, s, keeper, plane_both if s else None) for s in range(number)]
    aligned_spectra = aligned(spectra, tile_shifts)
    if whole_tiles:
        products = kernel_products(plane_both, received, packed)
    else:
        products = plain_products(plane_columns, received, packed)
    returned = [
        lax.all_to_all(block, "rows", split_axis=0, concat_axis=0, tiled=True)
        for block in products
    ]

    if whole_tiles:
        blocks = [block.reshape(tiles * groups, height, width) for block in returned]
        return (kernel_rows(blocks, inverse.reshape(TF2, TF2)), aligned_spectra)

    def to_rows(block):
        bins = block.reshape(tiles, groups, height, width)
        table = inverse.astype(np.float32)
        return jnp.einsum("bjrl,jln->rbn", bins, table, precision=full).reshape(height, breadth)

    correlation = jnp.stack([to_rows(block) for block in returned])
    return (correlation, aligned_spectra)


def solution(mesh):
    placed = (P("group", "rows", None), P("rows", None), P(), P("group", None, None))
    return jax.shard_map(
        per_device,
        mesh=mesh,
        in_specs=placed,
        out_specs=(P("group", "rows", None), P("group", "rows", None)),
        check_vma=False,
    )
```

```python
import math

import jax
import jax.numpy as jnp
import numpy as np
from jax import lax
from jax.experimental import pallas as pl
from jax.experimental.pallas import tpu as pltpu
from jax.sharding import PartitionSpec as P

F1 = 1024
TF2 = 512
HALF = TF2 // 2
MAXS = 8
LANES = 128

exact = lax.Precision.HIGH
full = lax.Precision.HIGHEST


def trig(rows, columns, modulus):
    angle = np.outer(np.arange(rows), np.arange(columns)) % modulus * (2.0 * math.pi / modulus)
    return np.cos(angle), np.sin(angle)


def column_table():
    return np.stack(trig(F1, F1, F1))


def row_tables(span):
    groups = HALF // span
    cosine, sine = trig(TF2, HALF, TF2)
    alternate = np.where(np.arange(TF2) % 2 == 0, 1.0, -1.0)
    forward_imag = -sine
    forward_imag[:, 0] = alternate
    forward = np.stack([cosine, forward_imag], axis=1)
    forward = forward.reshape(TF2, 2, groups, span).transpose(0, 2, 1, 3)
    forward = forward.reshape(TF2, groups, 2 * span)
    weights = np.where(np.arange(HALF) == 0, 1.0, 2.0)[None, :]
    inverse_imag = -2.0 * sine
    inverse_imag[:, 0] = alternate
    inverse = np.stack([weights * cosine, inverse_imag], axis=1)
    inverse = inverse.reshape(TF2, 2, groups, span).transpose(2, 1, 3, 0)
    inverse = inverse.reshape(groups, 2 * span, TF2) * float(F1 * TF2) ** (-1.5)
    return forward, inverse


def align_kernel(shifts, body, above, below, out, padded):
    spectrum = pl.program_id(0)
    height, breadth = body.shape[1:]
    total = height + 2 * MAXS
    margin = jnp.zeros((total, LANES), jnp.float32)
    padded[:, :LANES] = margin
    padded[:, LANES + breadth :] = margin
    padded[:MAXS, LANES : LANES + breadth] = above[0]
    padded[MAXS : MAXS + height, LANES : LANES + breadth] = body[0]
    padded[MAXS + height :, LANES : LANES + breadth] = below[0]
    window = TF2 + 2 * LANES
    for tile in range(breadth // TF2):
        down = shifts[spectrum, tile, 0]
        right = shifts[spectrum, tile, 1]
        part = padded[:, tile * TF2 : tile * TF2 + window]
        part = pltpu.roll(part, lax.rem(right + window, window), 1)[:, LANES : LANES + TF2]
        part = pltpu.roll(part, lax.rem(down + total, total), 0)
        out[0, :, tile * TF2 : (tile + 1) * TF2] = part[MAXS : MAXS + height]


def aligned(spectra, tile_shifts):
    number, height, breadth = spectra.shape
    count = lax.axis_size("rows")
    head = spectra[:, :MAXS]
    tail = spectra[:, height - MAXS :]
    above = lax.ppermute(tail, "rows", [(i, i + 1) for i in range(count - 1)])
    below = lax.ppermute(head, "rows", [(i + 1, i) for i in range(count - 1)])
    whole = pl.BlockSpec((1, height, breadth), lambda s: (s, 0, 0))
    edge = pl.BlockSpec((1, MAXS, breadth), lambda s: (s, 0, 0))
    return pl.pallas_call(
        align_kernel,
        grid=(number,),
        out_shape=jax.ShapeDtypeStruct(spectra.shape, jnp.float32),
        in_specs=[pl.BlockSpec(memory_space=pltpu.SMEM), whole, edge, edge],
        out_specs=whole,
        scratch_shapes=[pltpu.VMEM((height + 2 * MAXS, breadth + 2 * LANES), jnp.float32)],
        compiler_params=pltpu.CompilerParams(vmem_limit_bytes=24 * 2**20),
        cost_estimate=pl.CostEstimate(
            flops=20 * spectra.size, bytes_accessed=8 * spectra.size, transcendentals=0
        ),
    )(tile_shifts, spectra, above, below)


def plain_products(plane_columns, received, packed):
    count, local, height, width = plane_columns.shape
    span = width // 2
    columns = column_table().astype(np.float32)

    def halves(block):
        pencil = block.transpose(0, 2, 1, 3).reshape(F1, local * width)
        both = jnp.einsum("pkn,nl->pkl", columns, pencil, precision=exact)
        return both.reshape(2, F1, local, 2, span)

    def spectrum_of(both):
        cosine, sine = both[0], both[1]
        return cosine[:, :, 0] + sine[:, :, 1], cosine[:, :, 1] - sine[:, :, 0]

    plane_halves = halves(plane_columns)
    plane_real, plane_imag = spectrum_of(plane_halves)

    def back(block):
        both = halves(block)
        real, imag = spectrum_of(both)
        out_real = real * plane_real + imag * plane_imag
        out_imag = imag * plane_real - real * plane_imag
        cosine, sine = both[0], both[1]
        pc, ps = plane_halves[0], plane_halves[1]
        mask = packed[None, :, None, :]
        first = jnp.stack([out_real, out_imag], axis=2)
        second = jnp.stack([-out_imag, out_real], axis=2)
        first = jnp.where(mask, cosine * pc + sine * ps, first)
        second = jnp.where(mask, sine * pc - cosine * ps, second)
        pair = jnp.stack([first, second]).reshape(2, F1, local * width)
        rows = jnp.einsum("pkn,pnl->kl", columns, pair, precision=exact)
        return rows.reshape(count, height, local, width).transpose(0, 2, 1, 3)

    return [back(block) for block in received]


def split(values):
    high = values.astype(jnp.bfloat16)
    return high, (values - high.astype(jnp.float32)).astype(jnp.bfloat16)


def product_3(table_high, table_low, rows, high, low):
    def dot(a, b):
        return jnp.dot(a, b, preferred_element_type=jnp.float32)

    top = table_high[rows, :]
    return dot(top, high) + (dot(top, low) + dot(table_low[rows, :], high))


CHUNK = 256


def forward_halves(table_high, table_low, block, both, high, low):
    count, local, height, width = block.shape
    for source in range(count):
        for part in range(local):
            rows = slice(source * height, (source + 1) * height)
            lanes = slice(part * width, (part + 1) * width)
            high[rows, lanes], low[rows, lanes] = split(block[source, part])

    @pl.loop(0, 2 * F1 // CHUNK)
    def _(step):
        rows = pl.ds(pl.multiple_of(step * CHUNK, CHUNK), CHUNK)
        both[rows, :] = product_3(table_high, table_low, rows, high[...], low[...])


def product_kernel(
    table_high, table_low, block, plane_both, packed, out, both, high, low, pair_high, pair_low
):
    count, local, height, width = block.shape
    forward_halves(table_high, table_low, block, both, high, low)
    rows_per = 64
    lane = lax.broadcasted_iota(jnp.int32, (rows_per, width), 1)
    is_real = lane < width // 2
    sign = jnp.where(is_real, 1.0, -1.0).astype(jnp.float32)

    def swap(values):
        return pltpu.roll(values, width // 2, 1)

    @pl.loop(0, F1 // rows_per)
    def _(step):
        top = pl.ds(pl.multiple_of(step * rows_per, rows_per), rows_per)
        bottom = pl.ds(pl.multiple_of(F1 + step * rows_per, rows_per), rows_per)
        for part in range(local):
            lanes = slice(part * width, (part + 1) * width)
            c, s = both[top, lanes], both[bottom, lanes]
            pc, ps = plane_both[top, lanes], plane_both[bottom, lanes]
            value = c + sign * swap(s)
            plane_value = pc + sign * swap(ps)
            same = value * plane_value
            cross = swap(value) * plane_value
            product = jnp.where(is_real, same + swap(same), swap(cross) - cross)
            alone = packed[0:1, lanes] > 0.5
            first = jnp.where(alone, c * pc + s * ps, product)
            second = jnp.where(alone, s * pc - c * ps, -sign * swap(product))
            pair_high[top, lanes], pair_low[top, lanes] = split(first)
            pair_high[bottom, lanes], pair_low[bottom, lanes] = split(second)

    per_step = CHUNK // height

    @pl.loop(0, F1 // CHUNK)
    def _(step):
        total = jnp.zeros((CHUNK, local * width), jnp.float32)
        for side in range(2):
            rows = pl.ds(pl.multiple_of(side * F1 + step * CHUNK, CHUNK), CHUNK)
            own = slice(side * F1, (side + 1) * F1)
            total += product_3(table_high, table_low, rows, pair_high[own], pair_low[own])
        for place in range(per_step):
            for part in range(local):
                out[step * per_step + place, part] = total[
                    place * height : (place + 1) * height, part * width : (part + 1) * width
                ]


def column_parts():
    return split_table(column_table().reshape(2 * F1, F1))


def kernel_plane(plane_columns):
    breadth = plane_columns.shape[1] * plane_columns.shape[3]
    space = pl.BlockSpec(memory_space=pltpu.VMEM)
    return pl.pallas_call(
        forward_halves,
        out_shape=jax.ShapeDtypeStruct((2 * F1, breadth), jnp.float32),
        in_specs=[space] * 3,
        out_specs=space,
        scratch_shapes=[pltpu.VMEM((F1, breadth), jnp.bfloat16)] * 2,
        compiler_params=pltpu.CompilerParams(vmem_limit_bytes=44 * 2**20),
        cost_estimate=pl.CostEstimate(
            flops=12 * F1 * F1 * breadth, bytes_accessed=8 * F1 * F1, transcendentals=0
        ),
    )(*column_parts(), plane_columns)


def kernel_products(plane_both, received, packed):
    breadth = plane_both.shape[1]
    lanes = jnp.stack([packed, packed], axis=1).reshape(1, breadth).astype(jnp.float32)
    space = pl.BlockSpec(memory_space=pltpu.VMEM)
    halves_shape = (2 * F1, breadth)
    call = pl.pallas_call(
        product_kernel,
        out_shape=jax.ShapeDtypeStruct(received[0].shape, jnp.float32),
        in_specs=[space] * 5,
        out_specs=space,
        scratch_shapes=[pltpu.VMEM(halves_shape, jnp.float32)]
        + [pltpu.VMEM((F1, breadth), jnp.bfloat16)] * 2
        + [pltpu.VMEM(halves_shape, jnp.bfloat16)] * 2,
        compiler_params=pltpu.CompilerParams(vmem_limit_bytes=44 * 2**20),
        cost_estimate=pl.CostEstimate(
            flops=24 * F1 * F1 * breadth, bytes_accessed=8 * F1 * F1, transcendentals=0
        ),
    )
    return [call(*column_parts(), block, plane_both, lanes) for block in received]


def product_of(values, table_high, table_low):
    high, low = split(values)

    def dot(a, b):
        return jnp.dot(a, b, preferred_element_type=jnp.float32)

    count = values.shape[0]
    both = dot(jnp.concatenate([high, low], axis=0), table_high)
    return both[:count] + (both[count:] + dot(high, table_low))


def bins_kernel(keeper, rows, table_high, table_low, out):
    height, breadth = rows.shape
    groups = TF2 // LANES
    values = rows[...] * keeper[...]
    tiles = [values[:, start : start + TF2] for start in range(0, breadth, TF2)]
    bins = product_of(jnp.concatenate(tiles, axis=0), table_high[...], table_low[...])
    for tile in range(len(tiles)):
        for group in range(groups):
            out[tile * groups + group] = bins[
                tile * height : (tile + 1) * height, group * LANES : (group + 1) * LANES
            ]


def rows_kernel(*refs):
    blocks, (table_high, table_low, out) = refs[:-3], refs[-3:]
    granules, height = blocks[0].shape[:2]
    groups = TF2 // LANES
    places = [(s, t) for s in range(len(blocks)) for t in range(granules // groups)]
    parts = [
        jnp.concatenate([blocks[s][t * groups + group] for group in range(groups)], axis=1)
        for s, t in places
    ]
    rows = product_of(jnp.concatenate(parts, axis=0), table_high[...], table_low[...])
    for place, (s, t) in enumerate(places):
        out[s, :, t * TF2 : (t + 1) * TF2] = rows[place * height : (place + 1) * height]


def tiles_at_once(tiles):
    return 3 if tiles % 3 == 0 else 2 if tiles % 2 == 0 else 1


def split_table(table):
    high = table.astype(jnp.bfloat16)
    return high, (table - high.astype(np.float64)).astype(jnp.bfloat16)


def kernel_bins(spectra, index, keeper, table):
    height, breadth = spectra.shape[1:]
    tiles, groups = breadth // TF2, TF2 // LANES
    step = tiles_at_once(tiles)
    fixed = pl.BlockSpec((TF2, TF2), lambda b: (0, 0))
    return pl.pallas_call(
        bins_kernel,
        grid=(tiles // step,),
        out_shape=jax.ShapeDtypeStruct((tiles * groups, height, LANES), jnp.float32),
        in_specs=[
            pl.BlockSpec((1, step * TF2), lambda b: (0, b)),
            pl.BlockSpec((None, height, step * TF2), lambda b: (index, 0, b)),
            fixed,
            fixed,
        ],
        out_specs=pl.BlockSpec((step * groups, height, LANES), lambda b: (b, 0, 0)),
        compiler_params=pltpu.CompilerParams(vmem_limit_bytes=24 * 2**20),
        cost_estimate=pl.CostEstimate(
            flops=6 * height * breadth * TF2, bytes_accessed=8 * height * breadth, transcendentals=0
        ),
    )(keeper, spectra, *split_table(table))


def kernel_rows(blocks, table):
    granules, height = blocks[0].shape[:2]
    groups = TF2 // LANES
    tiles = granules // groups
    number = len(blocks)
    step = tiles_at_once(tiles)
    fixed = pl.BlockSpec((TF2, TF2), lambda b: (0, 0))
    return pl.pallas_call(
        rows_kernel,
        grid=(tiles // step,),
        out_shape=jax.ShapeDtypeStruct((number, height, tiles * TF2), jnp.float32),
        in_specs=[pl.BlockSpec((step * groups, height, LANES), lambda b: (b, 0, 0))] * number
        + [fixed, fixed],
        out_specs=pl.BlockSpec((number, height, step * TF2), lambda b: (0, 0, b)),
        compiler_params=pltpu.CompilerParams(vmem_limit_bytes=24 * 2**20),
    )(*blocks, *split_table(table))


FOLD = F1 // 2
TILE_GROUPS = TF2 // LANES
BLOCK = 256
STRIP = 64
QUAD = 4
MESH_ID = pl.DeviceIdType.MESH


def folded_table():
    cosine, sine = trig(FOLD, F1, F1)
    sine[0] = np.where(np.arange(F1) % 2 == 0, 1.0, -1.0)
    return np.concatenate([cosine, sine])


def swapped(values):
    return pltpu.roll(values, LANES // 2, 1)


def rows_of(bins, table_high, table_low, out, chunk):
    count, height = bins.shape[:2]
    tiles = count // TILE_GROUPS
    parts = [
        jnp.concatenate([bins[tile * TILE_GROUPS + group] for group in range(TILE_GROUPS)], axis=1)
        for tile in range(tiles)
    ]
    values = product_of(jnp.concatenate(parts, axis=0), table_high[...], table_low[...])
    for tile in range(tiles):
        start = (chunk * tiles + tile) * TF2
        out[:, start : start + TF2] = values[tile * height : (tile + 1) * height]


def last_kernel(
    aligned_in, done, bins, ready, last_high, last_low, correlation, aligned_out, fresh, sems
):
    width, late, last = done.shape[2], fresh.shape[1], bins.shape[0] - 1
    copies = [
        pltpu.make_async_copy(aligned_in, aligned_out, sems.at[0]),
        pltpu.make_async_copy(done, correlation.at[:, :, pl.ds(0, width)], sems.at[1]),
        pltpu.make_async_copy(
            ready, correlation.at[pl.ds(0, last), :, pl.ds(width, late)], sems.at[2]
        ),
        pltpu.make_async_copy(fresh, correlation.at[last, :, pl.ds(width, late)], sems.at[3]),
    ]
    for place, copy in enumerate(copies[:3]):
        copy.start(priority=place % 2)
    rows_of(bins.at[last], last_high, last_low, fresh, 0)
    copies[3].start()
    for copy in copies:
        copy.wait()


def whole_kernel(
    edges_in,
    shifts_in,
    spectra,
    plane,
    row_high_in,
    row_low_in,
    col_high_in,
    col_low_in,
    back_high_in,
    back_low_in,
    last_high_in,
    last_low_in,
    aligned_out,
    correlation,
    bins_last,
    fresh,
    last_high,
    last_low,
    edges,
    shifts,
    row_high,
    row_low,
    col_high,
    col_low,
    back_high,
    back_low,
    padded,
    plane_rows,
    plane_sent,
    plane_got,
    sent,
    got,
    returned,
    bins,
    coefs,
    both,
    high,
    low,
    pair_high,
    pair_low,
    load_sem,
    halo_send,
    halo_got,
    detour,
    detour_send,
    detour_got,
    plane_send_sem,
    plane_got_sem,
    swap_send_sem,
    swap_got_sem,
    spec_send_sem,
    spec_got_sem,
    back_send_sem,
    back_got_sem,
):
    number, height, breadth = spectra.shape
    count = lax.axis_size("rows")
    chunks = breadth // LANES // count
    per_chunk = count // TILE_GROUPS
    share = plane_rows.shape[0]
    me = lax.axis_index("rows")
    side = lax.axis_index("group")
    other = 1 - side
    middle = slice(LANES, LANES + breadth)

    barrier = pltpu.get_barrier_semaphore()

    def greet(step, carry):
        peer = lax.rem(me + step, count)
        pl.semaphore_signal(barrier, 1, device_id=(side, peer), device_id_type=MESH_ID)
        return carry

    lax.fori_loop(1, count, greet, 0)
    pl.semaphore_signal(barrier, 1, device_id=(other, me), device_id_type=MESH_ID)

    def load(source, target, sem):
        copy = pltpu.make_async_copy(source, target, load_sem.at[sem])
        copy.start()
        return copy

    own = pl.ds(pl.multiple_of(side * share, share), share)
    loads = [
        load(plane.at[own], plane_rows, 0),
        load(row_high_in, row_high, 1),
        load(row_low_in, row_low, 2),
        load(spectra, padded.at[:, pl.ds(MAXS, height), pl.ds(LANES, breadth)], 3),
        load(col_high_in, col_high, 4),
        load(col_low_in, col_low, 5),
        load(back_high_in, back_high, 6),
        load(back_low_in, back_low, 7),
        load(last_high_in, last_high, 8),
        load(last_low_in, last_low, 9),
        load(edges_in, edges, 10),
        load(shifts_in, shifts, 11),
    ]

    def remote(source, target, send, got_sem, where):
        return pltpu.make_async_remote_copy(
            src_ref=source,
            dst_ref=target,
            send_sem=send,
            recv_sem=got_sem,
            device_id=where,
            device_id_type=MESH_ID,
        )

    last = number - 1
    middle_low, middle_high = count // 2 - 1, count // 2
    senders, takers = (middle_low, middle_high), (middle_high, middle_low)
    detours = (middle_low - 2, middle_high + 2)
    outside = pl.ds(0, MAXS), pl.ds(MAXS + height, MAXS)
    inside_rows = pl.ds(height - MAXS, MAXS), pl.ds(0, MAXS)
    has_next = (me < count - 1, me > 0)
    has_previous = (me > 0, me < count - 1)

    def halo(way, which):
        kept = pl.ds(0, last) if which == 0 else pl.ds(last, 1)
        peer = lax.rem(me + (1, count - 1)[way], count)
        return remote(
            spectra.at[kept, inside_rows[way]],
            padded.at[kept, outside[way], pl.ds(LANES, breadth)],
            halo_send.at[way, which],
            halo_got.at[way, which],
            (side, peer),
        )

    def detour_out(way):
        return remote(
            spectra.at[pl.ds(last, 1), inside_rows[way]],
            detour.at[way],
            halo_send.at[way, 1],
            detour_got.at[way],
            (side, detours[way]),
        )

    def detour_on(way):
        return remote(
            detour.at[way],
            padded.at[pl.ds(last, 1), outside[way], pl.ds(LANES, breadth)],
            detour_send.at[way],
            halo_got.at[way, 1],
            (side, takers[way]),
        )

    def send_halos():
        for way in range(2):
            pl.when(has_next[way])(lambda: halo(way, 0).start())
            pl.when(has_next[way] & (me != senders[way]))(lambda: halo(way, 1).start())
            pl.when(me == senders[way])(lambda: detour_out(way).start())

    def pass_halos():
        for way in range(2):

            @pl.when(me == detours[way])
            def _():
                detour_out(way).wait_recv()
                detour_on(way).start()

    def take_halos():
        for way in range(2):
            for which in range(2):
                pl.when(has_previous[way])(lambda: halo(way, which).wait_recv())

    def finish_halos():
        for way in range(2):
            for which in range(2):
                pl.when(has_next[way])(lambda: halo(way, which).wait_send())
            pl.when(me == detours[way])(lambda: detour_on(way).wait_send())

    def to_all(start):
        def one(step, carry):
            half = lax.div(step + 1, 2)
            offset = count // 2 + half * (1 - 2 * lax.rem(step, 2))
            start(lax.rem(me + offset, count))
            return carry

        lax.fori_loop(0, count - 1, one, 0)

    def to_all_last(start):
        quad, place = lax.div(me, QUAD), lax.rem(me, QUAD)
        across = 2 * (1 - lax.div(quad, 2))
        for target in (across, across + 1, quad + 1 - 2 * lax.rem(quad, 2)):
            for turn in range(QUAD):
                start(target * QUAD + lax.rem(place + turn, QUAD))
        for turn in range(1, QUAD):
            start(quad * QUAD + lax.rem(place + turn, QUAD))

    column = lax.broadcasted_iota(jnp.int32, (1, TF2), 1)
    total = height + 2 * MAXS
    window = TF2 + 2 * LANES

    def landed(buffer, sem):
        fifteen = buffer.at[pl.ds(0, count - 1)]
        pltpu.make_async_copy(fifteen, fifteen, sem).wait()

    def swap_plane(chunk):
        half = plane_got.at[chunk, :, own]
        return remote(
            half, half, swap_send_sem.at[chunk], swap_got_sem.at[chunk], (other, me)
        )

    def transform(width):
        @pl.loop(0, F1 // BLOCK)
        def _(step):
            rows = pl.ds(pl.multiple_of(step * BLOCK, BLOCK), BLOCK)
            both[rows, :width] = product_3(
                col_high, col_low, rows, high[:, :width], low[:, :width]
            )

    lane = lax.broadcasted_iota(jnp.int32, (STRIP, LANES), 1)
    is_real = lane < LANES // 2
    first_row = lax.broadcasted_iota(jnp.int32, (STRIP, LANES), 0) == 0
    alone = (lax.rem(lane, LANES // 2) == 0) & (lax.rem(me, TILE_GROUPS) == 0)

    def strips(body):
        @pl.loop(0, FOLD // STRIP)
        def _(step):
            start = pl.multiple_of(step * STRIP, STRIP)
            body(pl.ds(start, STRIP), pl.ds(FOLD + start, STRIP))

    zero = jnp.zeros((STRIP, LANES), jnp.float32)

    def plane_coefs(chunk):
        def body(top, bottom):
            c, s = both[top, :LANES], both[bottom, :LANES]
            sc, ss = swapped(c), swapped(s)
            c2, s2 = c + c, s + s
            coefs[chunk, 0, top, :] = jnp.where(alone | is_real, c2, sc + sc)
            coefs[chunk, 1, top, :] = jnp.where(alone, zero, jnp.where(is_real, sc + sc, -c2))
            coefs[chunk, 2, top, :] = jnp.where(alone | is_real, s2, ss + ss)
            coefs[chunk, 3, top, :] = jnp.where(alone, zero, jnp.where(is_real, ss + ss, -s2))

        strips(body)

    def store_pair(rows, lanes, values, high_ref, low_ref):
        high_ref[rows, lanes], low_ref[rows, lanes] = split(values)

    def pairs(chunk):
        for spectrum in range(number):
            lanes = slice(spectrum * LANES, (spectrum + 1) * LANES)

            def take(top, bottom):
                c, s = both[top, lanes], both[bottom, lanes]
                sc, ss = swapped(c), swapped(s)
                a, d = coefs[chunk, 0, top, :], coefs[chunk, 1, top, :]
                f, b = coefs[chunk, 2, top, :], coefs[chunk, 3, top, :]
                return c, s, sc, ss, a, d, f, b

            def body(top, bottom):
                c, s, sc, ss, a, d, f, b = take(top, bottom)
                store_pair(top, lanes, (c * a + sc * d) + (s * f + ss * b), pair_high, pair_low)
                store_pair(bottom, lanes, (s * a + ss * d) - (c * f + sc * b), pair_high, pair_low)

            strips(body)
            top, bottom = pl.ds(0, STRIP), pl.ds(FOLD, STRIP)
            c, s, sc, ss, a, d, f, b = take(top, bottom)
            zeroth = 0.5 * (c * a + sc * d)
            nyquist = 0.5 * (s * f + ss * b)
            first = (c * a + sc * d) + (s * f + ss * b)
            second = (s * a + ss * d) - (c * f + sc * b)
            store_pair(top, lanes, jnp.where(first_row, zeroth, first), pair_high, pair_low)
            store_pair(bottom, lanes, jnp.where(first_row, nyquist, second), pair_high, pair_low)

    def gather(block, lanes):
        @pl.loop(0, count)
        def _(source):
            rows = pl.ds(pl.multiple_of(source * height, height), height)
            high[rows, lanes], low[rows, lanes] = split(block[source])
    held = BLOCK // height

    def send_plane_bins(chunk):
        tiles = [
            plane_rows[:, start : start + TF2]
            for start in range(chunk * per_chunk * TF2, (chunk + 1) * per_chunk * TF2, TF2)
        ]
        found = product_of(jnp.concatenate(tiles, axis=0), row_high[...], row_low[...])
        for tile in range(per_chunk):
            for group in range(TILE_GROUPS):
                plane_sent[chunk, tile * TILE_GROUPS + group] = found[
                    tile * share : (tile + 1) * share, group * LANES : (group + 1) * LANES
                ]
        plane_got[chunk, me, own] = plane_sent[chunk, me]

        if chunk == 0:
            pl.semaphore_wait(barrier, count)

        def send_plane(peer):
            remote(
                plane_sent.at[chunk, peer],
                plane_got.at[chunk, me, own],
                plane_send_sem.at[chunk],
                plane_got_sem.at[chunk],
                (side, peer),
            ).start()

        to_all(send_plane)

    def send_spectra_bins(chunk):
        def spectrum_bins(spectrum, carry):
            parts = []
            for tile in range(chunk * per_chunk, (chunk + 1) * per_chunk):
                inside = (column >= edges[0, tile]) & (column < TF2 - edges[1, tile])
                keeper = jnp.where(inside, 1.0, 0.0).astype(jnp.float32)
                lanes = slice(LANES + tile * TF2, LANES + (tile + 1) * TF2)
                parts.append(padded[spectrum, MAXS : MAXS + height, lanes] * keeper)
            found = product_of(jnp.concatenate(parts, axis=0), row_high[...], row_low[...])
            for tile in range(per_chunk):
                for group in range(TILE_GROUPS):
                    sent[chunk, spectrum, tile * TILE_GROUPS + group] = found[
                        tile * height : (tile + 1) * height, group * LANES : (group + 1) * LANES
                    ]
            got[chunk, spectrum, me] = sent[chunk, spectrum, me]

            def send_spectrum(peer):
                remote(
                    sent.at[chunk, spectrum, peer],
                    got.at[chunk, spectrum, me],
                    spec_send_sem.at[chunk, spectrum],
                    spec_got_sem.at[chunk, spectrum],
                    (side, peer),
                ).start()

            to_all(send_spectrum)
            return carry

        lax.fori_loop(0, number, spectrum_bins, 0)

    def align():
        margin = jnp.zeros((number, total, LANES), jnp.float32)
        padded[:, :, :LANES] = margin
        padded[:, :, LANES + breadth :] = margin
        blank = jnp.zeros((number, MAXS, breadth), jnp.float32)

        @pl.when(me == 0)
        def _():
            padded[:, :MAXS, middle] = blank

        @pl.when(me == count - 1)
        def _():
            padded[:, MAXS + height :, middle] = blank


        for spectrum in range(number):

            @pl.loop(0, breadth // TF2)
            def _(tile):
                down = shifts[spectrum, 0, tile]
                right = shifts[spectrum, 1, tile]
                start = pl.multiple_of(tile * TF2, TF2)
                part = padded[spectrum, :, pl.ds(start, window)]
                part = pltpu.roll(part, lax.rem(right + window, window), 1)[:, LANES : LANES + TF2]
                part = pltpu.roll(part, lax.rem(down + total, total), 0)
                aligned_out[spectrum, :, pl.ds(start, TF2)] = part[MAXS : MAXS + height]

    def exchange_plane(chunk):
        landed(plane_sent.at[chunk], plane_got_sem.at[chunk])
        swap_plane(chunk).start()

    def transform_plane(chunk):
        swapped_half = plane_got.at[chunk, :, pl.ds(pl.multiple_of(other * share, share), share)]
        pltpu.make_async_copy(swapped_half, swapped_half, swap_got_sem.at[chunk]).wait()
        gather(plane_got.at[chunk], slice(0, LANES))
        transform(LANES)
        plane_coefs(chunk)

    def multiply(chunk):
        for spectrum in range(number):
            landed(got.at[chunk, spectrum], spec_got_sem.at[chunk, spectrum])
            gather(got.at[chunk, spectrum], slice(spectrum * LANES, (spectrum + 1) * LANES))
        transform(number * LANES)
        pairs(chunk)
        target = bins.at[chunk] if chunk < chunks - 1 else bins_last

        def back(step, carry):
            place = step
            rows = pl.ds(pl.multiple_of(place * BLOCK, BLOCK), BLOCK)
            values = product_3(back_high, back_low, rows, pair_high[...], pair_low[...])
            for spectrum in range(number):
                for part in range(held):
                    returned[chunk, spectrum, place * held + part] = values[
                        part * height : (part + 1) * height,
                        spectrum * LANES : (spectrum + 1) * LANES,
                    ]

            return carry

        lax.fori_loop(0, count // held, back, 0)
        for spectrum in range(number):

            def send_back(peer):
                remote(
                    returned.at[chunk, spectrum, peer],
                    target.at[spectrum, me],
                    back_send_sem.at[chunk, spectrum],
                    back_got_sem.at[chunk, spectrum],
                    (side, peer),
                ).start()

            (to_all if chunk < chunks - 1 else to_all_last)(send_back)
            target[spectrum, me] = returned[chunk, spectrum, me]

    def finish_rows(chunk):
        for spectrum in range(number):
            landed(bins.at[chunk, spectrum], back_got_sem.at[chunk, spectrum])
            rows_of(bins.at[chunk, spectrum], last_high, last_low, correlation.at[spectrum], chunk)

    for load_index in (0, 1, 2):
        loads[load_index].wait()
    for chunk in range(chunks):
        send_plane_bins(chunk)
    for load_index in (3, 10, 11):
        loads[load_index].wait()
    send_spectra_bins(0)
    for chunk in range(chunks):
        exchange_plane(chunk)
    for chunk in range(1, chunks):
        send_spectra_bins(chunk)
        if chunk == 1:
            send_halos()
    for load_index in range(4, 10):
        loads[load_index].wait()
    for chunk in range(chunks):
        transform_plane(chunk)
    pass_halos()
    for chunk in range(chunks):
        multiply(chunk)
    take_halos()
    align()
    for chunk in range(chunks - 1):
        finish_rows(chunk)
    for spectrum in range(number):
        landed(bins_last.at[spectrum], back_got_sem.at[chunks - 1, spectrum])
        if spectrum < number - 1:
            rows_of(bins_last.at[spectrum], last_high, last_low, fresh.at[spectrum], 0)

    for chunk in range(chunks):
        landed(plane_sent.at[chunk], plane_send_sem.at[chunk])
        swap_plane(chunk).wait_send()
        for spectrum in range(number):
            landed(sent.at[chunk, spectrum], spec_send_sem.at[chunk, spectrum])
            landed(returned.at[chunk, spectrum], back_send_sem.at[chunk, spectrum])

    finish_halos()

def kernel_whole(spectra, plane, interval_edges, tile_shifts, forward, inverse):
    number, height, breadth = spectra.shape
    count = lax.axis_size("rows")
    share = height // lax.axis_size("group")
    chunks = breadth // LANES // count
    columns = folded_table()
    tables = (
        *split_table(forward),
        *split_table(columns),
        *split_table(np.ascontiguousarray(columns.T)),
        *split_table(inverse),
    )
    far = pl.BlockSpec(memory_space=pltpu.HBM)
    near = pl.BlockSpec(memory_space=pltpu.VMEM)
    breadths = (F1, number * LANES)
    blocks = (chunks, number, count, height, LANES)
    late = breadth // chunks
    held = (
        pltpu.VMEM(spectra.shape, jnp.float32),
        pltpu.VMEM((number, height, breadth - late), jnp.float32),
        pltpu.VMEM(blocks[1:], jnp.float32),
        pltpu.VMEM((number - 1, height, late), jnp.float32),
        pltpu.VMEM((TF2, TF2), jnp.bfloat16),
        pltpu.VMEM((TF2, TF2), jnp.bfloat16),
    )
    small = (interval_edges.T, tile_shifts.transpose(0, 2, 1))
    large = [
        pltpu.with_memory_space_constraint(value, pltpu.HBM)
        for value in (*small, spectra, plane, *map(jnp.asarray, tables))
    ]
    halfway = pl.pallas_call(
        whole_kernel,
        out_shape=held,
        in_specs=[far] * len(large),
        out_specs=(near,) * len(held),
        scratch_shapes=[pltpu.SMEM(value.shape, jnp.int32) for value in small]
        + [pltpu.VMEM(table.shape, jnp.bfloat16) for table in tables[:6]]
        + [
            pltpu.VMEM((number, height + 2 * MAXS, breadth + 2 * LANES), jnp.float32),
            pltpu.VMEM((share, breadth), jnp.float32),
            pltpu.VMEM((chunks, count, share, LANES), jnp.float32),
            pltpu.VMEM((chunks, count, height, LANES), jnp.float32),
            pltpu.VMEM(blocks, jnp.float32),
            pltpu.VMEM(blocks, jnp.float32),
            pltpu.VMEM(blocks, jnp.float32),
            pltpu.VMEM((chunks - 1,) + blocks[1:], jnp.float32),
            pltpu.VMEM((chunks, 4, FOLD, LANES), jnp.float32),
            pltpu.VMEM(breadths, jnp.float32),
            pltpu.VMEM(breadths, jnp.bfloat16),
            pltpu.VMEM(breadths, jnp.bfloat16),
            pltpu.VMEM(breadths, jnp.bfloat16),
            pltpu.VMEM(breadths, jnp.bfloat16),
            pltpu.SemaphoreType.DMA((12,)),
            pltpu.SemaphoreType.DMA((2, 2)),
            pltpu.SemaphoreType.DMA((2, 2)),
            pltpu.VMEM((2, 1, MAXS, breadth), jnp.float32),
            pltpu.SemaphoreType.DMA((2,)),
            pltpu.SemaphoreType.DMA((2,)),
            pltpu.SemaphoreType.DMA((chunks,)),
            pltpu.SemaphoreType.DMA((chunks,)),
            pltpu.SemaphoreType.DMA((chunks,)),
            pltpu.SemaphoreType.DMA((chunks,)),
            pltpu.SemaphoreType.DMA((chunks, number)),
            pltpu.SemaphoreType.DMA((chunks, number)),
            pltpu.SemaphoreType.DMA((chunks, number)),
            pltpu.SemaphoreType.DMA((chunks, number)),
        ],
        compiler_params=pltpu.CompilerParams(
            collective_id=0, has_side_effects=True, vmem_limit_bytes=44 * 2**20
        ),
        cost_estimate=pl.CostEstimate(
            flops=2 * 3 * F1 * F1 * (2 * number + 2) * chunks * LANES,
            bytes_accessed=16 * spectra.size,
            transcendentals=0,
        ),
    )(*large)
    whole = jax.ShapeDtypeStruct(spectra.shape, jnp.float32)
    return pl.pallas_call(
        last_kernel,
        out_shape=(whole, whole),
        in_specs=[near] * len(held),
        out_specs=(pl.BlockSpec(memory_space=pltpu.HBM),) * 2,
        scratch_shapes=[
            pltpu.VMEM((height, late), jnp.float32),
            pltpu.SemaphoreType.DMA((4,)),
        ],
        compiler_params=pltpu.CompilerParams(vmem_limit_bytes=16 * 2**20),
    )(*halfway)


def per_device(spectra, plane, interval_edges, tile_shifts):
    number, height, breadth = spectra.shape
    count = lax.axis_size("rows")
    tiles = breadth // TF2
    span = math.gcd(breadth // 2 // count, HALF)
    groups = HALF // span
    width = 2 * span
    local = tiles * groups // count
    forward, inverse = row_tables(span)

    point = jnp.arange(TF2, dtype=jnp.int32)[None, :]
    inside = (point >= interval_edges[:, 0:1]) & (point < TF2 - interval_edges[:, 1:2])
    keeper = jnp.where(inside, 1.0, 0.0).astype(jnp.float32).reshape(1, breadth)

    cohorts = lax.axis_size("group")
    share = height // cohorts
    whole_tiles = width == LANES and share % 16 == 0
    if whole_tiles and cohorts == 2 and height * count == F1 and count == QUAD * QUAD and number > 1:
        tables = (forward.reshape(TF2, TF2), inverse.reshape(TF2, TF2))
        return kernel_whole(spectra, plane, interval_edges, tile_shifts, *tables)

    def to_columns(rows, index, kept, after=None):
        held = rows.shape[1]
        if whole_tiles:
            bins = kernel_bins(rows, index, kept, forward.reshape(TF2, TF2))
        else:
            blocks = (rows[index] * kept).reshape(held, tiles, TF2)
            table = forward.astype(np.float32)
            bins = jnp.einsum("rbn,njl->bjrl", blocks, table, precision=full)
        sent = bins.reshape(count, local, held, width)
        if after is not None:
            sent, _ = lax.optimization_barrier((sent, after))
        return lax.all_to_all(sent, "rows", split_axis=0, concat_axis=0, tiled=True)

    granule = lax.axis_index("rows") * local + jnp.arange(local, dtype=jnp.int32)
    packed = (granule % groups == 0)[:, None] & (jnp.arange(span) == 0)[None, :]
    own = lax.axis_index("group")
    plane_rows = lax.dynamic_slice_in_dim(plane, own * share, share, axis=0)
    mine = to_columns(plane_rows[None], 0, jnp.ones_like(keeper))
    if cohorts == 2:
        other = lax.ppermute(mine, "group", [(0, 1), (1, 0)])
        ordered = [jnp.where(own == 0, mine, other), jnp.where(own == 0, other, mine)]
        plane_columns = jnp.concatenate(ordered, axis=2)
    else:
        plane_columns = lax.all_gather(mine, "group", axis=2, tiled=True)
    plane_both = kernel_plane(plane_columns) if whole_tiles else None
    received = [to_columns(spectra, s, keeper, plane_both if s else None) for s in range(number)]
    aligned_spectra = aligned(spectra, tile_shifts)
    if whole_tiles:
        products = kernel_products(plane_both, received, packed)
    else:
        products = plain_products(plane_columns, received, packed)
    returned = [
        lax.all_to_all(block, "rows", split_axis=0, concat_axis=0, tiled=True)
        for block in products
    ]

    if whole_tiles:
        blocks = [block.reshape(tiles * groups, height, width) for block in returned]
        return (kernel_rows(blocks, inverse.reshape(TF2, TF2)), aligned_spectra)

    def to_rows(block):
        bins = block.reshape(tiles, groups, height, width)
        table = inverse.astype(np.float32)
        return jnp.einsum("bjrl,jln->rbn", bins, table, precision=full).reshape(height, breadth)

    correlation = jnp.stack([to_rows(block) for block in returned])
    return (correlation, aligned_spectra)


def solution(mesh):
    placed = (P("group", "rows", None), P("rows", None), P(), P("group", None, None))
    return jax.shard_map(
        per_device,
        mesh=mesh,
        in_specs=placed,
        out_specs=(P("group", "rows", None), P("group", "rows", None)),
        check_vma=False,
    )
```

```python
import math

import jax
import jax.numpy as jnp
import numpy as np
from jax import lax
from jax.experimental import pallas as pl
from jax.experimental.pallas import tpu as pltpu
from jax.sharding import PartitionSpec as P

F1 = 1024
TF2 = 512
HALF = TF2 // 2
MAXS = 8
LANES = 128

exact = lax.Precision.HIGH
full = lax.Precision.HIGHEST


def trig(rows, columns, modulus):
    angle = np.outer(np.arange(rows), np.arange(columns)) % modulus * (2.0 * math.pi / modulus)
    return np.cos(angle), np.sin(angle)


def column_table():
    return np.stack(trig(F1, F1, F1))


def row_tables(span):
    groups = HALF // span
    cosine, sine = trig(TF2, HALF, TF2)
    alternate = np.where(np.arange(TF2) % 2 == 0, 1.0, -1.0)
    forward_imag = -sine
    forward_imag[:, 0] = alternate
    forward = np.stack([cosine, forward_imag], axis=1)
    forward = forward.reshape(TF2, 2, groups, span).transpose(0, 2, 1, 3)
    forward = forward.reshape(TF2, groups, 2 * span)
    weights = np.where(np.arange(HALF) == 0, 1.0, 2.0)[None, :]
    inverse_imag = -2.0 * sine
    inverse_imag[:, 0] = alternate
    inverse = np.stack([weights * cosine, inverse_imag], axis=1)
    inverse = inverse.reshape(TF2, 2, groups, span).transpose(2, 1, 3, 0)
    inverse = inverse.reshape(groups, 2 * span, TF2) * float(F1 * TF2) ** (-1.5)
    return forward, inverse


def align_kernel(shifts, body, above, below, out, padded):
    spectrum = pl.program_id(0)
    height, breadth = body.shape[1:]
    total = height + 2 * MAXS
    margin = jnp.zeros((total, LANES), jnp.float32)
    padded[:, :LANES] = margin
    padded[:, LANES + breadth :] = margin
    padded[:MAXS, LANES : LANES + breadth] = above[0]
    padded[MAXS : MAXS + height, LANES : LANES + breadth] = body[0]
    padded[MAXS + height :, LANES : LANES + breadth] = below[0]
    window = TF2 + 2 * LANES
    for tile in range(breadth // TF2):
        down = shifts[spectrum, tile, 0]
        right = shifts[spectrum, tile, 1]
        part = padded[:, tile * TF2 : tile * TF2 + window]
        part = pltpu.roll(part, lax.rem(right + window, window), 1)[:, LANES : LANES + TF2]
        part = pltpu.roll(part, lax.rem(down + total, total), 0)
        out[0, :, tile * TF2 : (tile + 1) * TF2] = part[MAXS : MAXS + height]


def aligned(spectra, tile_shifts):
    number, height, breadth = spectra.shape
    count = lax.axis_size("rows")
    head = spectra[:, :MAXS]
    tail = spectra[:, height - MAXS :]
    above = lax.ppermute(tail, "rows", [(i, i + 1) for i in range(count - 1)])
    below = lax.ppermute(head, "rows", [(i + 1, i) for i in range(count - 1)])
    whole = pl.BlockSpec((1, height, breadth), lambda s: (s, 0, 0))
    edge = pl.BlockSpec((1, MAXS, breadth), lambda s: (s, 0, 0))
    return pl.pallas_call(
        align_kernel,
        grid=(number,),
        out_shape=jax.ShapeDtypeStruct(spectra.shape, jnp.float32),
        in_specs=[pl.BlockSpec(memory_space=pltpu.SMEM), whole, edge, edge],
        out_specs=whole,
        scratch_shapes=[pltpu.VMEM((height + 2 * MAXS, breadth + 2 * LANES), jnp.float32)],
        compiler_params=pltpu.CompilerParams(vmem_limit_bytes=24 * 2**20),
        cost_estimate=pl.CostEstimate(
            flops=20 * spectra.size, bytes_accessed=8 * spectra.size, transcendentals=0
        ),
    )(tile_shifts, spectra, above, below)


def plain_products(plane_columns, received, packed):
    count, local, height, width = plane_columns.shape
    span = width // 2
    columns = column_table().astype(np.float32)

    def halves(block):
        pencil = block.transpose(0, 2, 1, 3).reshape(F1, local * width)
        both = jnp.einsum("pkn,nl->pkl", columns, pencil, precision=exact)
        return both.reshape(2, F1, local, 2, span)

    def spectrum_of(both):
        cosine, sine = both[0], both[1]
        return cosine[:, :, 0] + sine[:, :, 1], cosine[:, :, 1] - sine[:, :, 0]

    plane_halves = halves(plane_columns)
    plane_real, plane_imag = spectrum_of(plane_halves)

    def back(block):
        both = halves(block)
        real, imag = spectrum_of(both)
        out_real = real * plane_real + imag * plane_imag
        out_imag = imag * plane_real - real * plane_imag
        cosine, sine = both[0], both[1]
        pc, ps = plane_halves[0], plane_halves[1]
        mask = packed[None, :, None, :]
        first = jnp.stack([out_real, out_imag], axis=2)
        second = jnp.stack([-out_imag, out_real], axis=2)
        first = jnp.where(mask, cosine * pc + sine * ps, first)
        second = jnp.where(mask, sine * pc - cosine * ps, second)
        pair = jnp.stack([first, second]).reshape(2, F1, local * width)
        rows = jnp.einsum("pkn,pnl->kl", columns, pair, precision=exact)
        return rows.reshape(count, height, local, width).transpose(0, 2, 1, 3)

    return [back(block) for block in received]


def split(values):
    high = values.astype(jnp.bfloat16)
    return high, (values - high.astype(jnp.float32)).astype(jnp.bfloat16)


def product_3(table_high, table_low, rows, high, low):
    def dot(a, b):
        return jnp.dot(a, b, preferred_element_type=jnp.float32)

    top = table_high[rows, :]
    return dot(top, high) + (dot(top, low) + dot(table_low[rows, :], high))


CHUNK = 256


def forward_halves(table_high, table_low, block, both, high, low):
    count, local, height, width = block.shape
    for source in range(count):
        for part in range(local):
            rows = slice(source * height, (source + 1) * height)
            lanes = slice(part * width, (part + 1) * width)
            high[rows, lanes], low[rows, lanes] = split(block[source, part])

    @pl.loop(0, 2 * F1 // CHUNK)
    def _(step):
        rows = pl.ds(pl.multiple_of(step * CHUNK, CHUNK), CHUNK)
        both[rows, :] = product_3(table_high, table_low, rows, high[...], low[...])


def product_kernel(
    table_high, table_low, block, plane_both, packed, out, both, high, low, pair_high, pair_low
):
    count, local, height, width = block.shape
    forward_halves(table_high, table_low, block, both, high, low)
    rows_per = 64
    lane = lax.broadcasted_iota(jnp.int32, (rows_per, width), 1)
    is_real = lane < width // 2
    sign = jnp.where(is_real, 1.0, -1.0).astype(jnp.float32)

    def swap(values):
        return pltpu.roll(values, width // 2, 1)

    @pl.loop(0, F1 // rows_per)
    def _(step):
        top = pl.ds(pl.multiple_of(step * rows_per, rows_per), rows_per)
        bottom = pl.ds(pl.multiple_of(F1 + step * rows_per, rows_per), rows_per)
        for part in range(local):
            lanes = slice(part * width, (part + 1) * width)
            c, s = both[top, lanes], both[bottom, lanes]
            pc, ps = plane_both[top, lanes], plane_both[bottom, lanes]
            value = c + sign * swap(s)
            plane_value = pc + sign * swap(ps)
            same = value * plane_value
            cross = swap(value) * plane_value
            product = jnp.where(is_real, same + swap(same), swap(cross) - cross)
            alone = packed[0:1, lanes] > 0.5
            first = jnp.where(alone, c * pc + s * ps, product)
            second = jnp.where(alone, s * pc - c * ps, -sign * swap(product))
            pair_high[top, lanes], pair_low[top, lanes] = split(first)
            pair_high[bottom, lanes], pair_low[bottom, lanes] = split(second)

    per_step = CHUNK // height

    @pl.loop(0, F1 // CHUNK)
    def _(step):
        total = jnp.zeros((CHUNK, local * width), jnp.float32)
        for side in range(2):
            rows = pl.ds(pl.multiple_of(side * F1 + step * CHUNK, CHUNK), CHUNK)
            own = slice(side * F1, (side + 1) * F1)
            total += product_3(table_high, table_low, rows, pair_high[own], pair_low[own])
        for place in range(per_step):
            for part in range(local):
                out[step * per_step + place, part] = total[
                    place * height : (place + 1) * height, part * width : (part + 1) * width
                ]


def column_parts():
    return split_table(column_table().reshape(2 * F1, F1))


def kernel_plane(plane_columns):
    breadth = plane_columns.shape[1] * plane_columns.shape[3]
    space = pl.BlockSpec(memory_space=pltpu.VMEM)
    return pl.pallas_call(
        forward_halves,
        out_shape=jax.ShapeDtypeStruct((2 * F1, breadth), jnp.float32),
        in_specs=[space] * 3,
        out_specs=space,
        scratch_shapes=[pltpu.VMEM((F1, breadth), jnp.bfloat16)] * 2,
        compiler_params=pltpu.CompilerParams(vmem_limit_bytes=44 * 2**20),
        cost_estimate=pl.CostEstimate(
            flops=12 * F1 * F1 * breadth, bytes_accessed=8 * F1 * F1, transcendentals=0
        ),
    )(*column_parts(), plane_columns)


def kernel_products(plane_both, received, packed):
    breadth = plane_both.shape[1]
    lanes = jnp.stack([packed, packed], axis=1).reshape(1, breadth).astype(jnp.float32)
    space = pl.BlockSpec(memory_space=pltpu.VMEM)
    halves_shape = (2 * F1, breadth)
    call = pl.pallas_call(
        product_kernel,
        out_shape=jax.ShapeDtypeStruct(received[0].shape, jnp.float32),
        in_specs=[space] * 5,
        out_specs=space,
        scratch_shapes=[pltpu.VMEM(halves_shape, jnp.float32)]
        + [pltpu.VMEM((F1, breadth), jnp.bfloat16)] * 2
        + [pltpu.VMEM(halves_shape, jnp.bfloat16)] * 2,
        compiler_params=pltpu.CompilerParams(vmem_limit_bytes=44 * 2**20),
        cost_estimate=pl.CostEstimate(
            flops=24 * F1 * F1 * breadth, bytes_accessed=8 * F1 * F1, transcendentals=0
        ),
    )
    return [call(*column_parts(), block, plane_both, lanes) for block in received]


def product_of(values, table_high, table_low):
    high, low = split(values)

    def dot(a, b):
        return jnp.dot(a, b, preferred_element_type=jnp.float32)

    count = values.shape[0]
    both = dot(jnp.concatenate([high, low], axis=0), table_high)
    return both[:count] + (both[count:] + dot(high, table_low))


def bins_kernel(keeper, rows, table_high, table_low, out):
    height, breadth = rows.shape
    groups = TF2 // LANES
    values = rows[...] * keeper[...]
    tiles = [values[:, start : start + TF2] for start in range(0, breadth, TF2)]
    bins = product_of(jnp.concatenate(tiles, axis=0), table_high[...], table_low[...])
    for tile in range(len(tiles)):
        for group in range(groups):
            out[tile * groups + group] = bins[
                tile * height : (tile + 1) * height, group * LANES : (group + 1) * LANES
            ]


def rows_kernel(*refs):
    blocks, (table_high, table_low, out) = refs[:-3], refs[-3:]
    granules, height = blocks[0].shape[:2]
    groups = TF2 // LANES
    places = [(s, t) for s in range(len(blocks)) for t in range(granules // groups)]
    parts = [
        jnp.concatenate([blocks[s][t * groups + group] for group in range(groups)], axis=1)
        for s, t in places
    ]
    rows = product_of(jnp.concatenate(parts, axis=0), table_high[...], table_low[...])
    for place, (s, t) in enumerate(places):
        out[s, :, t * TF2 : (t + 1) * TF2] = rows[place * height : (place + 1) * height]


def tiles_at_once(tiles):
    return 3 if tiles % 3 == 0 else 2 if tiles % 2 == 0 else 1


def split_table(table):
    high = table.astype(jnp.bfloat16)
    return high, (table - high.astype(np.float64)).astype(jnp.bfloat16)


def kernel_bins(spectra, index, keeper, table):
    height, breadth = spectra.shape[1:]
    tiles, groups = breadth // TF2, TF2 // LANES
    step = tiles_at_once(tiles)
    fixed = pl.BlockSpec((TF2, TF2), lambda b: (0, 0))
    return pl.pallas_call(
        bins_kernel,
        grid=(tiles // step,),
        out_shape=jax.ShapeDtypeStruct((tiles * groups, height, LANES), jnp.float32),
        in_specs=[
            pl.BlockSpec((1, step * TF2), lambda b: (0, b)),
            pl.BlockSpec((None, height, step * TF2), lambda b: (index, 0, b)),
            fixed,
            fixed,
        ],
        out_specs=pl.BlockSpec((step * groups, height, LANES), lambda b: (b, 0, 0)),
        compiler_params=pltpu.CompilerParams(vmem_limit_bytes=24 * 2**20),
        cost_estimate=pl.CostEstimate(
            flops=6 * height * breadth * TF2, bytes_accessed=8 * height * breadth, transcendentals=0
        ),
    )(keeper, spectra, *split_table(table))


def kernel_rows(blocks, table):
    granules, height = blocks[0].shape[:2]
    groups = TF2 // LANES
    tiles = granules // groups
    number = len(blocks)
    step = tiles_at_once(tiles)
    fixed = pl.BlockSpec((TF2, TF2), lambda b: (0, 0))
    return pl.pallas_call(
        rows_kernel,
        grid=(tiles // step,),
        out_shape=jax.ShapeDtypeStruct((number, height, tiles * TF2), jnp.float32),
        in_specs=[pl.BlockSpec((step * groups, height, LANES), lambda b: (b, 0, 0))] * number
        + [fixed, fixed],
        out_specs=pl.BlockSpec((number, height, step * TF2), lambda b: (0, 0, b)),
        compiler_params=pltpu.CompilerParams(vmem_limit_bytes=24 * 2**20),
    )(*blocks, *split_table(table))


FOLD = F1 // 2
TILE_GROUPS = TF2 // LANES
BLOCK = 256
STRIP = 64
QUAD = 4
MESH_ID = pl.DeviceIdType.MESH


def folded_table():
    cosine, sine = trig(FOLD, F1, F1)
    sine[0] = np.where(np.arange(F1) % 2 == 0, 1.0, -1.0)
    return np.concatenate([cosine, sine])


def swapped(values):
    return pltpu.roll(values, LANES // 2, 1)


def rows_of(bins, table_high, table_low, out, chunk):
    count, height = bins.shape[:2]
    tiles = count // TILE_GROUPS
    parts = [
        jnp.concatenate([bins[tile * TILE_GROUPS + group] for group in range(TILE_GROUPS)], axis=1)
        for tile in range(tiles)
    ]
    values = product_of(jnp.concatenate(parts, axis=0), table_high[...], table_low[...])
    for tile in range(tiles):
        start = (chunk * tiles + tile) * TF2
        out[:, start : start + TF2] = values[tile * height : (tile + 1) * height]


def last_kernel(
    aligned_in, done, bins, ready, last_high, last_low, correlation, aligned_out, fresh, sems
):
    width, late, last = done.shape[2], fresh.shape[1], bins.shape[0] - 1
    copies = [
        pltpu.make_async_copy(aligned_in, aligned_out, sems.at[0]),
        pltpu.make_async_copy(done, correlation.at[:, :, pl.ds(0, width)], sems.at[1]),
        pltpu.make_async_copy(
            ready, correlation.at[pl.ds(0, last), :, pl.ds(width, late)], sems.at[2]
        ),
        pltpu.make_async_copy(fresh, correlation.at[last, :, pl.ds(width, late)], sems.at[3]),
    ]
    for place, copy in enumerate(copies[:3]):
        copy.start(priority=place % 2)
    rows_of(bins.at[last], last_high, last_low, fresh, 0)
    copies[3].start()
    for copy in copies:
        copy.wait()


def whole_kernel(
    edges_in,
    shifts_in,
    spectra,
    plane,
    row_high_in,
    row_low_in,
    col_high_in,
    col_low_in,
    back_high_in,
    back_low_in,
    last_high_in,
    last_low_in,
    aligned_out,
    correlation,
    bins_last,
    fresh,
    last_high,
    last_low,
    edges,
    shifts,
    row_high,
    row_low,
    col_high,
    col_low,
    back_high,
    back_low,
    padded,
    plane_rows,
    plane_sent,
    plane_got,
    sent,
    got,
    returned,
    bins,
    coefs,
    both,
    high,
    low,
    pair_high,
    pair_low,
    load_sem,
    halo_send,
    halo_got,
    detour,
    detour_send,
    detour_got,
    plane_send_sem,
    plane_got_sem,
    swap_send_sem,
    swap_got_sem,
    spec_send_sem,
    spec_got_sem,
    back_send_sem,
    back_got_sem,
):
    number, height, breadth = spectra.shape
    count = lax.axis_size("rows")
    chunks = breadth // LANES // count
    per_chunk = count // TILE_GROUPS
    share = plane_rows.shape[0]
    me = lax.axis_index("rows")
    side = lax.axis_index("group")
    other = 1 - side
    middle = slice(LANES, LANES + breadth)

    barrier = pltpu.get_barrier_semaphore()

    def greet(step, carry):
        peer = lax.rem(me + step, count)
        pl.semaphore_signal(barrier, 1, device_id=(side, peer), device_id_type=MESH_ID)
        return carry

    lax.fori_loop(1, count, greet, 0)
    pl.semaphore_signal(barrier, 1, device_id=(other, me), device_id_type=MESH_ID)

    def load(source, target, sem):
        copy = pltpu.make_async_copy(source, target, load_sem.at[sem])
        copy.start()
        return copy

    own = pl.ds(pl.multiple_of(side * share, share), share)
    loads = [
        load(plane.at[own], plane_rows, 0),
        load(row_high_in, row_high, 1),
        load(row_low_in, row_low, 2),
        load(spectra, padded.at[:, pl.ds(MAXS, height), pl.ds(LANES, breadth)], 3),
        load(col_high_in, col_high, 4),
        load(col_low_in, col_low, 5),
        load(back_high_in, back_high, 6),
        load(back_low_in, back_low, 7),
        load(last_high_in, last_high, 8),
        load(last_low_in, last_low, 9),
        load(edges_in, edges, 10),
        load(shifts_in, shifts, 11),
    ]

    def remote(source, target, send, got_sem, where):
        return pltpu.make_async_remote_copy(
            src_ref=source,
            dst_ref=target,
            send_sem=send,
            recv_sem=got_sem,
            device_id=where,
            device_id_type=MESH_ID,
        )

    last = number - 1
    middle_low, middle_high = count // 2 - 1, count // 2
    senders, takers = (middle_low, middle_high), (middle_high, middle_low)
    detours = (middle_low - 2, middle_high + 2)
    outside = pl.ds(0, MAXS), pl.ds(MAXS + height, MAXS)
    inside_rows = pl.ds(height - MAXS, MAXS), pl.ds(0, MAXS)
    has_next = (me < count - 1, me > 0)
    has_previous = (me > 0, me < count - 1)

    def halo(way, which):
        kept = pl.ds(0, last) if which == 0 else pl.ds(last, 1)
        peer = lax.rem(me + (1, count - 1)[way], count)
        return remote(
            spectra.at[kept, inside_rows[way]],
            padded.at[kept, outside[way], pl.ds(LANES, breadth)],
            halo_send.at[way, which],
            halo_got.at[way, which],
            (side, peer),
        )

    def detour_out(way):
        return remote(
            spectra.at[pl.ds(last, 1), inside_rows[way]],
            detour.at[way],
            halo_send.at[way, 1],
            detour_got.at[way],
            (side, detours[way]),
        )

    def detour_on(way):
        return remote(
            detour.at[way],
            padded.at[pl.ds(last, 1), outside[way], pl.ds(LANES, breadth)],
            detour_send.at[way],
            halo_got.at[way, 1],
            (side, takers[way]),
        )

    def send_halos():
        for way in range(2):
            pl.when(has_next[way])(lambda: halo(way, 0).start())
            pl.when(has_next[way] & (me != senders[way]))(lambda: halo(way, 1).start())
            pl.when(me == senders[way])(lambda: detour_out(way).start())

    def pass_halos():
        for way in range(2):

            @pl.when(me == detours[way])
            def _():
                detour_out(way).wait_recv()
                detour_on(way).start()

    def take_halos():
        for way in range(2):
            for which in range(2):
                pl.when(has_previous[way])(lambda: halo(way, which).wait_recv())

    def finish_halos():
        for way in range(2):
            for which in range(2):
                pl.when(has_next[way])(lambda: halo(way, which).wait_send())
            pl.when(me == detours[way])(lambda: detour_on(way).wait_send())

    def to_all(start):
        def one(step, carry):
            half = lax.div(step + 1, 2)
            offset = count // 2 + half * (1 - 2 * lax.rem(step, 2))
            start(lax.rem(me + offset, count))
            return carry

        lax.fori_loop(0, count - 1, one, 0)

    def to_all_last(start):
        quad, place = lax.div(me, QUAD), lax.rem(me, QUAD)
        across = 2 * (1 - lax.div(quad, 2))
        for target in (quad + 1 - 2 * lax.rem(quad, 2), quad, across, across + 1):
            for turn in range(QUAD):
                if target is quad and turn == 0:
                    continue
                start(target * QUAD + lax.rem(place + turn, QUAD))

    column = lax.broadcasted_iota(jnp.int32, (1, TF2), 1)
    total = height + 2 * MAXS
    window = TF2 + 2 * LANES

    def landed(buffer, sem):
        fifteen = buffer.at[pl.ds(0, count - 1)]
        pltpu.make_async_copy(fifteen, fifteen, sem).wait()

    def swap_plane(chunk):
        half = plane_got.at[chunk, :, own]
        return remote(
            half, half, swap_send_sem.at[chunk], swap_got_sem.at[chunk], (other, me)
        )

    def transform(width):
        @pl.loop(0, F1 // BLOCK)
        def _(step):
            rows = pl.ds(pl.multiple_of(step * BLOCK, BLOCK), BLOCK)
            both[rows, :width] = product_3(
                col_high, col_low, rows, high[:, :width], low[:, :width]
            )

    lane = lax.broadcasted_iota(jnp.int32, (STRIP, LANES), 1)
    is_real = lane < LANES // 2
    first_row = lax.broadcasted_iota(jnp.int32, (STRIP, LANES), 0) == 0
    alone = (lax.rem(lane, LANES // 2) == 0) & (lax.rem(me, TILE_GROUPS) == 0)

    def strips(body):
        @pl.loop(0, FOLD // STRIP)
        def _(step):
            start = pl.multiple_of(step * STRIP, STRIP)
            body(pl.ds(start, STRIP), pl.ds(FOLD + start, STRIP))

    zero = jnp.zeros((STRIP, LANES), jnp.float32)

    def plane_coefs(chunk):
        def body(top, bottom):
            c, s = both[top, :LANES], both[bottom, :LANES]
            sc, ss = swapped(c), swapped(s)
            c2, s2 = c + c, s + s
            coefs[chunk, 0, top, :] = jnp.where(alone | is_real, c2, sc + sc)
            coefs[chunk, 1, top, :] = jnp.where(alone, zero, jnp.where(is_real, sc + sc, -c2))
            coefs[chunk, 2, top, :] = jnp.where(alone | is_real, s2, ss + ss)
            coefs[chunk, 3, top, :] = jnp.where(alone, zero, jnp.where(is_real, ss + ss, -s2))

        strips(body)

    def store_pair(rows, lanes, values, high_ref, low_ref):
        high_ref[rows, lanes], low_ref[rows, lanes] = split(values)

    def pairs(chunk):
        for spectrum in range(number):
            lanes = slice(spectrum * LANES, (spectrum + 1) * LANES)

            def take(top, bottom):
                c, s = both[top, lanes], both[bottom, lanes]
                sc, ss = swapped(c), swapped(s)
                a, d = coefs[chunk, 0, top, :], coefs[chunk, 1, top, :]
                f, b = coefs[chunk, 2, top, :], coefs[chunk, 3, top, :]
                return c, s, sc, ss, a, d, f, b

            def body(top, bottom):
                c, s, sc, ss, a, d, f, b = take(top, bottom)
                store_pair(top, lanes, (c * a + sc * d) + (s * f + ss * b), pair_high, pair_low)
                store_pair(bottom, lanes, (s * a + ss * d) - (c * f + sc * b), pair_high, pair_low)

            strips(body)
            top, bottom = pl.ds(0, STRIP), pl.ds(FOLD, STRIP)
            c, s, sc, ss, a, d, f, b = take(top, bottom)
            zeroth = 0.5 * (c * a + sc * d)
            nyquist = 0.5 * (s * f + ss * b)
            first = (c * a + sc * d) + (s * f + ss * b)
            second = (s * a + ss * d) - (c * f + sc * b)
            store_pair(top, lanes, jnp.where(first_row, zeroth, first), pair_high, pair_low)
            store_pair(bottom, lanes, jnp.where(first_row, nyquist, second), pair_high, pair_low)

    def gather(block, lanes):
        @pl.loop(0, count)
        def _(source):
            rows = pl.ds(pl.multiple_of(source * height, height), height)
            high[rows, lanes], low[rows, lanes] = split(block[source])
    held = BLOCK // height

    def send_plane_bins(chunk):
        tiles = [
            plane_rows[:, start : start + TF2]
            for start in range(chunk * per_chunk * TF2, (chunk + 1) * per_chunk * TF2, TF2)
        ]
        found = product_of(jnp.concatenate(tiles, axis=0), row_high[...], row_low[...])
        for tile in range(per_chunk):
            for group in range(TILE_GROUPS):
                plane_sent[chunk, tile * TILE_GROUPS + group] = found[
                    tile * share : (tile + 1) * share, group * LANES : (group + 1) * LANES
                ]
        plane_got[chunk, me, own] = plane_sent[chunk, me]

        if chunk == 0:
            pl.semaphore_wait(barrier, count)

        def send_plane(peer):
            remote(
                plane_sent.at[chunk, peer],
                plane_got.at[chunk, me, own],
                plane_send_sem.at[chunk],
                plane_got_sem.at[chunk],
                (side, peer),
            ).start()

        to_all(send_plane)

    def send_spectra_bins(chunk):
        def spectrum_bins(spectrum, carry):
            parts = []
            for tile in range(chunk * per_chunk, (chunk + 1) * per_chunk):
                inside = (column >= edges[0, tile]) & (column < TF2 - edges[1, tile])
                keeper = jnp.where(inside, 1.0, 0.0).astype(jnp.float32)
                lanes = slice(LANES + tile * TF2, LANES + (tile + 1) * TF2)
                parts.append(padded[spectrum, MAXS : MAXS + height, lanes] * keeper)
            found = product_of(jnp.concatenate(parts, axis=0), row_high[...], row_low[...])
            for tile in range(per_chunk):
                for group in range(TILE_GROUPS):
                    sent[chunk, spectrum, tile * TILE_GROUPS + group] = found[
                        tile * height : (tile + 1) * height, group * LANES : (group + 1) * LANES
                    ]
            got[chunk, spectrum, me] = sent[chunk, spectrum, me]

            def send_spectrum(peer):
                remote(
                    sent.at[chunk, spectrum, peer],
                    got.at[chunk, spectrum, me],
                    spec_send_sem.at[chunk, spectrum],
                    spec_got_sem.at[chunk, spectrum],
                    (side, peer),
                ).start()

            to_all(send_spectrum)
            return carry

        lax.fori_loop(0, number, spectrum_bins, 0)

    def align():
        margin = jnp.zeros((number, total, LANES), jnp.float32)
        padded[:, :, :LANES] = margin
        padded[:, :, LANES + breadth :] = margin
        blank = jnp.zeros((number, MAXS, breadth), jnp.float32)

        @pl.when(me == 0)
        def _():
            padded[:, :MAXS, middle] = blank

        @pl.when(me == count - 1)
        def _():
            padded[:, MAXS + height :, middle] = blank


        for spectrum in range(number):

            @pl.loop(0, breadth // TF2)
            def _(tile):
                down = shifts[spectrum, 0, tile]
                right = shifts[spectrum, 1, tile]
                start = pl.multiple_of(tile * TF2, TF2)
                part = padded[spectrum, :, pl.ds(start, window)]
                part = pltpu.roll(part, lax.rem(right + window, window), 1)[:, LANES : LANES + TF2]
                part = pltpu.roll(part, lax.rem(down + total, total), 0)
                aligned_out[spectrum, :, pl.ds(start, TF2)] = part[MAXS : MAXS + height]

    def exchange_plane(chunk):
        landed(plane_sent.at[chunk], plane_got_sem.at[chunk])
        swap_plane(chunk).start()

    def transform_plane(chunk):
        swapped_half = plane_got.at[chunk, :, pl.ds(pl.multiple_of(other * share, share), share)]
        pltpu.make_async_copy(swapped_half, swapped_half, swap_got_sem.at[chunk]).wait()
        gather(plane_got.at[chunk], slice(0, LANES))
        transform(LANES)
        plane_coefs(chunk)

    def multiply(chunk):
        for spectrum in range(number):
            landed(got.at[chunk, spectrum], spec_got_sem.at[chunk, spectrum])
            gather(got.at[chunk, spectrum], slice(spectrum * LANES, (spectrum + 1) * LANES))
        transform(number * LANES)
        pairs(chunk)
        target = bins.at[chunk] if chunk < chunks - 1 else bins_last

        def back(step, carry):
            place = step
            rows = pl.ds(pl.multiple_of(place * BLOCK, BLOCK), BLOCK)
            values = product_3(back_high, back_low, rows, pair_high[...], pair_low[...])
            for spectrum in range(number):
                for part in range(held):
                    returned[chunk, spectrum, place * held + part] = values[
                        part * height : (part + 1) * height,
                        spectrum * LANES : (spectrum + 1) * LANES,
                    ]

            return carry

        lax.fori_loop(0, count // held, back, 0)
        for spectrum in range(number):

            def send_back(peer):
                remote(
                    returned.at[chunk, spectrum, peer],
                    target.at[spectrum, me],
                    back_send_sem.at[chunk, spectrum],
                    back_got_sem.at[chunk, spectrum],
                    (side, peer),
                ).start()

            (to_all if chunk < chunks - 1 else to_all_last)(send_back)
            target[spectrum, me] = returned[chunk, spectrum, me]

    def finish_rows(chunk):
        for spectrum in range(number):
            landed(bins.at[chunk, spectrum], back_got_sem.at[chunk, spectrum])
            rows_of(bins.at[chunk, spectrum], last_high, last_low, correlation.at[spectrum], chunk)

    for load_index in (0, 1, 2):
        loads[load_index].wait()
    for chunk in range(chunks):
        send_plane_bins(chunk)
    for load_index in (3, 10, 11):
        loads[load_index].wait()
    send_spectra_bins(0)
    for chunk in range(chunks):
        exchange_plane(chunk)
    for chunk in range(1, chunks):
        send_spectra_bins(chunk)
        if chunk == 1:
            send_halos()
    for load_index in range(4, 10):
        loads[load_index].wait()
    for chunk in range(chunks):
        transform_plane(chunk)
    pass_halos()
    for chunk in range(chunks):
        multiply(chunk)
    take_halos()
    align()
    for chunk in range(chunks - 1):
        finish_rows(chunk)
    for spectrum in range(number):
        landed(bins_last.at[spectrum], back_got_sem.at[chunks - 1, spectrum])
        if spectrum < number - 1:
            rows_of(bins_last.at[spectrum], last_high, last_low, fresh.at[spectrum], 0)

    for chunk in range(chunks):
        landed(plane_sent.at[chunk], plane_send_sem.at[chunk])
        swap_plane(chunk).wait_send()
        for spectrum in range(number):
            landed(sent.at[chunk, spectrum], spec_send_sem.at[chunk, spectrum])
            landed(returned.at[chunk, spectrum], back_send_sem.at[chunk, spectrum])

    finish_halos()

def kernel_whole(spectra, plane, interval_edges, tile_shifts, forward, inverse):
    number, height, breadth = spectra.shape
    count = lax.axis_size("rows")
    share = height // lax.axis_size("group")
    chunks = breadth // LANES // count
    columns = folded_table()
    tables = (
        *split_table(forward),
        *split_table(columns),
        *split_table(np.ascontiguousarray(columns.T)),
        *split_table(inverse),
    )
    far = pl.BlockSpec(memory_space=pltpu.HBM)
    near = pl.BlockSpec(memory_space=pltpu.VMEM)
    breadths = (F1, number * LANES)
    blocks = (chunks, number, count, height, LANES)
    late = breadth // chunks
    held = (
        pltpu.VMEM(spectra.shape, jnp.float32),
        pltpu.VMEM((number, height, breadth - late), jnp.float32),
        pltpu.VMEM(blocks[1:], jnp.float32),
        pltpu.VMEM((number - 1, height, late), jnp.float32),
        pltpu.VMEM((TF2, TF2), jnp.bfloat16),
        pltpu.VMEM((TF2, TF2), jnp.bfloat16),
    )
    small = (interval_edges.T, tile_shifts.transpose(0, 2, 1))
    large = [
        pltpu.with_memory_space_constraint(value, pltpu.HBM)
        for value in (*small, spectra, plane, *map(jnp.asarray, tables))
    ]
    halfway = pl.pallas_call(
        whole_kernel,
        out_shape=held,
        in_specs=[far] * len(large),
        out_specs=(near,) * len(held),
        scratch_shapes=[pltpu.SMEM(value.shape, jnp.int32) for value in small]
        + [pltpu.VMEM(table.shape, jnp.bfloat16) for table in tables[:6]]
        + [
            pltpu.VMEM((number, height + 2 * MAXS, breadth + 2 * LANES), jnp.float32),
            pltpu.VMEM((share, breadth), jnp.float32),
            pltpu.VMEM((chunks, count, share, LANES), jnp.float32),
            pltpu.VMEM((chunks, count, height, LANES), jnp.float32),
            pltpu.VMEM(blocks, jnp.float32),
            pltpu.VMEM(blocks, jnp.float32),
            pltpu.VMEM(blocks, jnp.float32),
            pltpu.VMEM((chunks - 1,) + blocks[1:], jnp.float32),
            pltpu.VMEM((chunks, 4, FOLD, LANES), jnp.float32),
            pltpu.VMEM(breadths, jnp.float32),
            pltpu.VMEM(breadths, jnp.bfloat16),
            pltpu.VMEM(breadths, jnp.bfloat16),
            pltpu.VMEM(breadths, jnp.bfloat16),
            pltpu.VMEM(breadths, jnp.bfloat16),
            pltpu.SemaphoreType.DMA((12,)),
            pltpu.SemaphoreType.DMA((2, 2)),
            pltpu.SemaphoreType.DMA((2, 2)),
            pltpu.VMEM((2, 1, MAXS, breadth), jnp.float32),
            pltpu.SemaphoreType.DMA((2,)),
            pltpu.SemaphoreType.DMA((2,)),
            pltpu.SemaphoreType.DMA((chunks,)),
            pltpu.SemaphoreType.DMA((chunks,)),
            pltpu.SemaphoreType.DMA((chunks,)),
            pltpu.SemaphoreType.DMA((chunks,)),
            pltpu.SemaphoreType.DMA((chunks, number)),
            pltpu.SemaphoreType.DMA((chunks, number)),
            pltpu.SemaphoreType.DMA((chunks, number)),
            pltpu.SemaphoreType.DMA((chunks, number)),
        ],
        compiler_params=pltpu.CompilerParams(
            collective_id=0, has_side_effects=True, vmem_limit_bytes=44 * 2**20
        ),
        cost_estimate=pl.CostEstimate(
            flops=2 * 3 * F1 * F1 * (2 * number + 2) * chunks * LANES,
            bytes_accessed=16 * spectra.size,
            transcendentals=0,
        ),
    )(*large)
    whole = jax.ShapeDtypeStruct(spectra.shape, jnp.float32)
    return pl.pallas_call(
        last_kernel,
        out_shape=(whole, whole),
        in_specs=[near] * len(held),
        out_specs=(pl.BlockSpec(memory_space=pltpu.HBM),) * 2,
        scratch_shapes=[
            pltpu.VMEM((height, late), jnp.float32),
            pltpu.SemaphoreType.DMA((4,)),
        ],
        compiler_params=pltpu.CompilerParams(vmem_limit_bytes=16 * 2**20),
    )(*halfway)


def per_device(spectra, plane, interval_edges, tile_shifts):
    number, height, breadth = spectra.shape
    count = lax.axis_size("rows")
    tiles = breadth // TF2
    span = math.gcd(breadth // 2 // count, HALF)
    groups = HALF // span
    width = 2 * span
    local = tiles * groups // count
    forward, inverse = row_tables(span)

    point = jnp.arange(TF2, dtype=jnp.int32)[None, :]
    inside = (point >= interval_edges[:, 0:1]) & (point < TF2 - interval_edges[:, 1:2])
    keeper = jnp.where(inside, 1.0, 0.0).astype(jnp.float32).reshape(1, breadth)

    cohorts = lax.axis_size("group")
    share = height // cohorts
    whole_tiles = width == LANES and share % 16 == 0
    if whole_tiles and cohorts == 2 and height * count == F1 and count == QUAD * QUAD and number > 1:
        tables = (forward.reshape(TF2, TF2), inverse.reshape(TF2, TF2))
        return kernel_whole(spectra, plane, interval_edges, tile_shifts, *tables)

    def to_columns(rows, index, kept, after=None):
        held = rows.shape[1]
        if whole_tiles:
            bins = kernel_bins(rows, index, kept, forward.reshape(TF2, TF2))
        else:
            blocks = (rows[index] * kept).reshape(held, tiles, TF2)
            table = forward.astype(np.float32)
            bins = jnp.einsum("rbn,njl->bjrl", blocks, table, precision=full)
        sent = bins.reshape(count, local, held, width)
        if after is not None:
            sent, _ = lax.optimization_barrier((sent, after))
        return lax.all_to_all(sent, "rows", split_axis=0, concat_axis=0, tiled=True)

    granule = lax.axis_index("rows") * local + jnp.arange(local, dtype=jnp.int32)
    packed = (granule % groups == 0)[:, None] & (jnp.arange(span) == 0)[None, :]
    own = lax.axis_index("group")
    plane_rows = lax.dynamic_slice_in_dim(plane, own * share, share, axis=0)
    mine = to_columns(plane_rows[None], 0, jnp.ones_like(keeper))
    if cohorts == 2:
        other = lax.ppermute(mine, "group", [(0, 1), (1, 0)])
        ordered = [jnp.where(own == 0, mine, other), jnp.where(own == 0, other, mine)]
        plane_columns = jnp.concatenate(ordered, axis=2)
    else:
        plane_columns = lax.all_gather(mine, "group", axis=2, tiled=True)
    plane_both = kernel_plane(plane_columns) if whole_tiles else None
    received = [to_columns(spectra, s, keeper, plane_both if s else None) for s in range(number)]
    aligned_spectra = aligned(spectra, tile_shifts)
    if whole_tiles:
        products = kernel_products(plane_both, received, packed)
    else:
        products = plain_products(plane_columns, received, packed)
    returned = [
        lax.all_to_all(block, "rows", split_axis=0, concat_axis=0, tiled=True)
        for block in products
    ]

    if whole_tiles:
        blocks = [block.reshape(tiles * groups, height, width) for block in returned]
        return (kernel_rows(blocks, inverse.reshape(TF2, TF2)), aligned_spectra)

    def to_rows(block):
        bins = block.reshape(tiles, groups, height, width)
        table = inverse.astype(np.float32)
        return jnp.einsum("bjrl,jln->rbn", bins, table, precision=full).reshape(height, breadth)

    correlation = jnp.stack([to_rows(block) for block in returned])
    return (correlation, aligned_spectra)


def solution(mesh):
    placed = (P("group", "rows", None), P("rows", None), P(), P("group", None, None))
    return jax.shard_map(
        per_device,
        mesh=mesh,
        in_specs=placed,
        out_specs=(P("group", "rows", None), P("group", "rows", None)),
        check_vma=False,
    )
```
